32 devices in a mesh: gx: 4 (over z), gy: 8 (over y, x, core).
Axes of the slice: x: 2, y: 2, z: 4, core: 2. Of those that a mesh axis runs over, the one named last changes fastest.
Arguments:
- scalars: float32 [4, 64, 64, 1024], P(None, None, 'gx', 'gy'), may hold values from -6 to 6
- winds: float32 [2, 64, 64, 1024], P(None, None, 'gx', 'gy'), may hold values from -0.6 to 0.6
- map_factor: float32 [64, 1024], P('gx', 'gy'), may hold values from 0.7 to 1.3
- urban_counts: int32 [32], P(('gx', 'gy')), may hold values from 64 to 256, as said below
- urban_cols: int32 [8192], P(('gx', 'gy')), may hold values from 0 to 2047, as said below
- street_class: int32 [8192], P(('gx', 'gy')), may hold values from 0 to 9
- area_table: float32 [10, 10], replicated, may hold values from 0.2 to 1
- wall_temp: float32 [10, 8192], P(None, ('gx', 'gy')), may hold values from -6 to 6
- indoor_temp: float32 [8192], P(('gx', 'gy')), may hold values from -6 to 6
Outputs:
- scalars_out: float32 [4, 64, 64, 1024], P(None, None, 'gx', 'gy')
- wall_out: float32 [10, 8192], P(None, ('gx', 'gy'))
- indoor_out: float32 [8192], P(('gx', 'gy'))
The draws below stay inside these ranges and needn't reach their ends.
Inputs may be any that keep to these rules, and one draw needn't show every extreme that they name: `urban_counts`: some tile has exactly 256 live urban columns. `urban_cols`: the 256 entries of each tile are distinct cells of that tile, numbered x * 128 + y within it.
All inputs are finite; a program needn't handle non-finite values.
Results may differ from the reference program's by a relative error of at most 0.000056.
Values sent between devices are 32-bit elements; how exact they have to be, the bound alone decides.
No kernel may reach another device: no remote copies, remote signals or barrier semaphores. Data moves between devices by JAX's collectives and lax.ppermute only.
A program may use at most 192 MiB of HBM per device.

```python
import jax
import jax.numpy as jnp
from jax import lax

CX = 16
CY = 128
LEV = 64
NSC = 4
UL = 10
NWL = 10
NCLS = 10
CAP = 256
NX = 64
NY = 1024
N_GY = 8
DEVICES = 32


def draw_urban_counts(key, part):
    counts = jax.random.randint(key, (DEVICES,), CAP // 4, CAP + 1)
    chosen = jax.random.randint(jax.random.fold_in(key, 7), (), 0, DEVICES)
    return counts.at[chosen].set(CAP).astype(jnp.int32)


def draw_urban_cols(key, part):
    keys = jax.random.split(key, DEVICES)

    def one_tile(tile_key):
        return jax.random.permutation(tile_key, CX * CY)[:CAP]
    return jax.vmap(one_tile)(keys).reshape(-1).astype(jnp.int32)


def plant(values, own_key, least, top_value):
    shape = values.shape
    spot = [jax.random.randint(jax.random.fold_in(own_key, axis), (), 0, shape[axis]) for axis in range(len(shape))]
    values = values.at[tuple(spot)].set(least)
    longest = shape.index(max(shape))
    spot[longest] = (spot[longest] + 1) % shape[longest]
    return values.at[tuple(spot)].set(top_value)


def block_scale(stream_key, shape, cuts, smallest, high):
    factor_of, own = 1.0, jax.random.fold_in(stream_key, 6)
    for axis_at, parts in cuts:
        draws = jnp.exp(jax.random.uniform(jax.random.fold_in(own, axis_at), (parts,), jnp.float32, smallest / len(cuts), high / len(cuts)))
        factor_of = factor_of * jnp.repeat(draws, shape[axis_at] // parts).reshape([-1 if axis == axis_at else 1 for axis in range(len(shape))])
    return factor_of


def gaussian(key, dims, spread, bound, shards=(), kind=jnp.bfloat16):
    drawn = jax.random.normal(key, dims, jnp.float32) * spread
    if len(shards) > 0:
        drawn = block_scale(key, dims, shards, -0.22, 0.18) * drawn
    return jnp.clip(drawn, min=-bound, max=bound).astype(kind)


def setup_inputs(seed: int = 0) -> dict:
    key_of = jax.random.split(jax.random.key(seed), 10)
    scalars = gaussian(key_of[0], (NSC, LEV, NX, NY), 1.0, 6.0, ((2, 4), (3, 8)), jnp.float32)
    winds = jnp.clip(jax.random.uniform(key_of[1], (2, LEV, NX, NY), jnp.float32, -0.6, 0.6) * block_scale(key_of[1], (2, LEV, NX, NY), ((2, 4), (3, 8)), -0.4, 0.0), -0.6, 0.6)
    map_factor = jnp.clip(1.0 + 0.06 * jax.random.normal(key_of[2], (NX, NY), jnp.float32), 0.7, 1.3)
    urban_counts = draw_urban_counts(jax.random.fold_in(key_of[9], 71), 0)
    urban_cols = draw_urban_cols(jax.random.fold_in(key_of[9], 71), 0)
    street_class = plant(jax.random.randint(key_of[5], (DEVICES * CAP,), 0, NCLS), jax.random.fold_in(key_of[5], 1), 0, NCLS - 1).astype(jnp.int32)
    area_table = jnp.clip(jax.random.uniform(key_of[6], (NCLS, UL), jnp.float32, 0.2, 1.0), 0.2, 1.0)
    wall_temp = gaussian(key_of[7], (NWL, DEVICES * CAP), 1.0, 6.0, ((1, 32),), jnp.float32)
    indoor_temp = gaussian(key_of[8], (DEVICES * CAP,), 1.0, 6.0, ((0, 32),), jnp.float32)
    return dict(scalars=scalars, winds=winds, map_factor=map_factor, urban_counts=urban_counts, urban_cols=urban_cols, street_class=street_class, area_table=area_table, wall_temp=wall_temp, indoor_temp=indoor_temp)


heat_coef = 0.5
wall_coef = 0.05
conduct = 0.3
inner_coef = 0.2
room_coef = 0.1
flux_coef = 0.5


def face_divergence(field, speed, axis):
    shifted = [jnp.roll(field, -(offset - 2), axis) for offset in range(6)]
    face_speed = 0.5 * (speed + jnp.roll(speed, -1, axis))
    flux = face_speed * (37.0 * (shifted[2] + shifted[3]) - 8.0 * (shifted[1] + shifted[4]) + (shifted[0] + shifted[5])) / 60.0
    flux = flux - jnp.abs(face_speed) * ((shifted[5] - shifted[0]) - 5.0 * (shifted[4] - shifted[1]) + 10.0 * (shifted[3] - shifted[2])) / 60.0
    return flux - jnp.roll(flux, 1, axis)


def physics(packed):
    air_temp = packed[:UL]
    areas = packed[UL:2 * UL]
    walls = packed[2 * UL:2 * UL + NWL]
    indoor = packed[2 * UL + NWL]
    heat = heat_coef * areas * (walls[0] - air_temp)
    first = walls[0] - wall_coef * jnp.sum(heat, axis=0) + conduct * (walls[1] - walls[0])
    middle = walls[1:-1] + conduct * (walls[:-2] - 2.0 * walls[1:-1] + walls[2:])
    last = walls[-1] + conduct * (walls[-2] - walls[-1]) + inner_coef * (indoor - walls[-1])
    indoor_new = indoor + room_coef * (walls[-1] - indoor)
    return jnp.concatenate([heat, first[None], middle, last[None], indoor_new[None]], axis=0)


def reference(scalars, winds, map_factor, urban_counts, urban_cols, street_class, area_table, wall_temp, indoor_temp):
    square = map_factor * map_factor

    def tendency(field):
        return -square * (face_divergence(field, winds[0], 1) + face_divergence(field, winds[1], 2))

    def advance(field):
        section_one = field + tendency(field) / 3.0
        section_two = field + tendency(section_one) / 2.0
        return field + tendency(section_two)

    advanced = lax.map(advance, scalars)
    device = jnp.arange(DEVICES, dtype=jnp.int32)
    row_tile = (device // N_GY)[:, None]
    col_tile = (device % N_GY)[:, None]
    cells = urban_cols.reshape(DEVICES, CAP)
    west = row_tile * CX + cells // CY
    south = col_tile * CY + cells % CY
    flat = (west * NY + south).reshape(-1).astype(jnp.int32)
    lower = advanced[0, :UL].reshape(UL, NX * NY)
    air_temp = lower[:, flat]
    areas = area_table.T[:, street_class]
    packed = jnp.concatenate([air_temp, areas, wall_temp, indoor_temp[None]], axis=0)
    result = physics(packed)
    live = (jnp.arange(CAP, dtype=jnp.int32)[None, :] < urban_counts[:, None]).reshape(-1)
    heating = jnp.where(live[None, :], flux_coef * result[:UL], 0.0)
    lower = lower.at[:, flat].add(heating).reshape(UL, NX, NY)
    scalars_out = advanced.at[0, :UL].set(lower)
    wall_out = jnp.where(live[None, :], result[UL:UL + NWL], wall_temp)
    indoor_out = jnp.where(live, result[UL + NWL], indoor_temp)
    return (scalars_out, wall_out, indoor_out)
```

```python
import functools

import jax
import jax.numpy as jnp
from jax import lax
from jax.experimental import pallas as pl
from jax.experimental.pallas import tpu as pltpu
from jax.sharding import PartitionSpec as P

UL = 10
NWL = 10
NCLS = 10
WIDTH = 3
GROUP = 8
CHUNKS = 2

heat_coef = 0.5
wall_coef = 0.05
conduct = 0.3
inner_coef = 0.2
room_coef = 0.1
flux_coef = 0.5
face_scale = 0.5 / 60.0


def lane_index(shape):
    return lax.broadcasted_iota(jnp.int32, shape, 1)


def rolled(array, shift):
    return pltpu.roll(array, shift % array.shape[1], 1)


def pack_edges(packed, row, x):
    moved = rolled(row, GROUP * x + WIDTH)
    lane = lane_index(row.shape)
    here = (lane >= GROUP * x) & (lane < GROUP * x + 2 * WIDTH)
    return moved if packed is None else jnp.where(here, moved, packed)


def ahead(row, halo, lane, k):
    if k > 0:
        return rolled(jnp.where(lane < k, halo, row), -k)
    return rolled(jnp.where(lane >= row.shape[1] + k, halo, row), -k)


def combine(a, b, c, d, e, f, speed):
    high = 37.0 * (c + d) - 8.0 * (b + e) + (a + f)
    damp = (f - a) - 5.0 * (e - b) + 10.0 * (d - c)
    return speed * high - jnp.abs(speed) * damp


def extract_kernel(tiles, x_size, with_wind, *refs):
    if with_wind:
        field, wind, low, high, packed = refs
    else:
        field, low, high, packed = refs
    rows = field.shape[0] // x_size

    def one(t, carry):
        base = pl.multiple_of(t * 8 * x_size, 8 * x_size)
        edges = None
        for x in range(x_size):
            row = field[pl.ds(base + x, 8, stride=x_size), :]
            if x < WIDTH:
                low[pl.ds(pl.multiple_of(x * rows + t * 8, 8), 8), :] = row
            if x >= x_size - WIDTH:
                at = (x - x_size + WIDTH) * rows
                high[pl.ds(pl.multiple_of(at + t * 8, 8), 8), :] = row
            edges = pack_edges(edges, row, x)
        packed[pl.ds(pl.multiple_of(t * 8, 8), 8), :] = edges
        return carry

    lax.fori_loop(0, rows // 8, one, 0)
    if with_wind:
        levels = wind.shape[0] // (2 * x_size)

        def one_wind(t, carry):
            base = pl.multiple_of(t * 8 * x_size, 8 * x_size)
            at = pl.ds(pl.multiple_of(WIDTH * rows + t * 8, 8), 8)
            low[at, :] = wind[pl.ds(base, 8, stride=x_size), :]
            high[at, :] = wind[pl.ds(base + x_size - 1, 8, stride=x_size), :]
            base = base + levels * x_size
            edges = None
            for x in range(x_size):
                edges = pack_edges(edges, wind[pl.ds(base + x, 8, stride=x_size), :], x)
            packed[pl.ds(pl.multiple_of(rows + t * 8, 8), 8), :] = edges
            return carry

        lax.fori_loop(0, levels // 8, one_wind, 0)


def wind_kernel(x_size, wind, west, east, south, north, own, speed_x, speed_y, speed_edge):
    levels = speed_x.shape[1]

    def one(t, carry):
        base = pl.multiple_of(t * 8 * x_size, 8 * x_size)
        at = pl.ds(pl.multiple_of(t * 8, 8), 8)
        before = west[at, :]
        for x in range(x_size + 1):
            now = east[at, :] if x == x_size else wind[pl.ds(base + x, 8, stride=x_size), :]
            speed_x[x, at, :] = face_scale * (before + now)
            before = now
        base = base + levels * x_size
        lane = lane_index(before.shape)
        first = (lane & (GROUP - 1)) < WIDTH
        halo = jnp.where(first, south[at, :], north[at, :])
        for x in range(x_size):
            row = wind[pl.ds(base + x, 8, stride=x_size), :]
            edge = rolled(halo, -(GROUP * x + WIDTH))
            speed_y[x, at, :] = face_scale * (row + ahead(row, edge, lane, 1))
        seam = jnp.where(first, south[at, :], own[at, :])
        speed_edge[at, :] = face_scale * (seam + rolled(seam, -1))
        return carry

    lax.fori_loop(0, levels // 8, one, 0)


def section_tile(t, x_size, divisor, load, base, halos, packs, speeds, factor, store):
    west, east = halos
    south, north, own = packs
    speed_x, speed_y, speed_edge = speeds
    at = pl.ds(pl.multiple_of(t * 8, 8), 8)
    south_edges = south[at, :]
    lane = lane_index(south_edges.shape)
    first = (lane & (GROUP - 1)) < WIDTH
    halo = jnp.where(first, south_edges, north[at, :])
    seam = jnp.where(first, south_edges, own[at, :])
    seam_flux = combine(*[rolled(seam, -k) for k in range(-2, 4)], speed_edge[at, :])

    def cell(x):
        if x < 0:
            return west[x + WIDTH][at, :]
        if x >= x_size:
            return east[x - x_size][at, :]
        return load(x, at)

    q = [cell(x) for x in range(-3, 2)]
    d1 = [q[i + 1] - q[i] for i in range(4)]
    d2 = [d1[i + 1] - d1[i] for i in range(3)]
    d3 = [d2[i + 1] - d2[i] for i in range(2)]
    d4 = d3[1] - d3[0]
    smooth = d4 - 5.0 * d2[1] + 30.0 * q[2]
    flux_before = None
    q, d1, d2, d3 = q[3:], d1[-1], d2[-1], d3[-1]
    edges = None
    for x in range(-1, x_size):
        q.append(cell(x + WIDTH))
        new1 = q[-1] - q[-2]
        new2 = new1 - d1
        new3 = new2 - d2
        new4 = new3 - d3
        new_smooth = new4 - 5.0 * d2 + 30.0 * q[0]
        speed = speed_x[x + 1, at, :]
        flux = speed * (smooth + new_smooth) - jnp.abs(speed) * (new4 - d4)
        d1, d2, d3, d4, smooth = new1, new2, new3, new4, new_smooth
        if x >= 0:
            row = row_here
            edge = rolled(halo, -(GROUP * x + WIDTH))
            around = [row if k == 0 else ahead(row, edge, lane, k) for k in range(-2, 4)]
            flux_y = combine(*around, speed_y[x, at, :])
            entry = rolled(seam_flux, -(GROUP * x + 2))
            below = jnp.where(lane == 0, entry, rolled(flux_y, 1))
            divergence = (flux - flux_before) + (flux_y - below)
            mapped = factor[pl.ds(x, 1), :]
            scale = mapped * mapped * (-1.0 / divisor)
            new = base(x) + scale * divergence
            store(x, at, new)
            edges = pack_edges(edges, new, x)
        flux_before = flux
        row_here = q[0]
        q = q[1:]
    return edges


def section_kernel(x_size, divisor, first, last, with_city, *refs):
    refs = list(refs)
    section = refs.pop(0)
    base_ref = section if first else refs.pop(0)
    west = [refs.pop(0) for _ in range(WIDTH)]
    east = [refs.pop(0) for _ in range(WIDTH)]
    south, north, own = [refs.pop(0) for _ in range(3)]
    speed_x, speed_y, speed_edge, factor = [refs.pop(0) for _ in range(4)]
    rows = south.shape[0]

    def strided(ref, t, x):
        start = pl.multiple_of(t * 8 * x_size, 8 * x_size)
        return ref.at[pl.ds(start + x, 8, stride=x_size), :]

    if last:
        if with_city:
            city = [refs.pop(0) for _ in range(6)]
            out, wall_out, indoor_out = refs
        else:
            refs.pop(0)
            (out,) = refs
    else:
        out, low, high, packed = refs

    def one(t, carry):
        def load(x, at):
            if first:
                return section[pl.ds(pl.multiple_of(t * 8 * x_size, 8 * x_size) + x, 8, stride=x_size), :]
            return section[x, at, :]

        def base(x):
            return base_ref[pl.ds(pl.multiple_of(t * 8 * x_size, 8 * x_size) + x, 8, stride=x_size), :]

        def store(x, at, new):
            if last:
                out[pl.ds(pl.multiple_of(t * 8 * x_size, 8 * x_size) + x, 8, stride=x_size), :] = new
                return
            out[x, at, :] = new
            if x < WIDTH:
                low[x, at, :] = new
            if x >= x_size - WIDTH:
                high[x - x_size + WIDTH, at, :] = new

        edges = section_tile(
            t, x_size, divisor, load, base, (west, east), (south, north, own), (speed_x, speed_y, speed_edge), factor, store
        )
        if not last:
            packed[pl.ds(pl.multiple_of(t * 8, 8), 8), :] = edges
        return carry

    lax.fori_loop(0, rows // 8, one, 0)
    if last and with_city:

        @pl.when(pl.program_id(0) == 0)
        def _():
            city_step(x_size, out, *city, wall_out, indoor_out)


def dot(a, b, dims):
    return lax.dot_general(
        a, b, (dims, ((), ())), precision=lax.Precision.HIGHEST, preferred_element_type=jnp.float32
    )


def city_step(x_size, out, counts, cols_ref, class_ref, table, wall_ref, indoor_ref, wall_out, indoor_out):
    deep = 16
    cols = cols_ref[...]
    slots = cols.shape[1]
    y_size = out.shape[1]
    cell_x = lax.div(cols, y_size)
    cell_y = lax.rem(cols, y_size)
    lower = [
        jnp.concatenate([out[pl.ds(8 * x_size * t + x, 8, stride=x_size), :] for t in range(deep // 8)], axis=0)
        for x in range(x_size)
    ]
    at_y = (lax.broadcasted_iota(jnp.int32, (y_size, slots), 0) == cell_y).astype(jnp.float32)
    gathered = dot(jnp.concatenate(lower, axis=0), at_y, ((1,), (0,)))
    air = jnp.zeros((deep, slots), jnp.float32)
    for x in range(x_size):
        air = jnp.where(cell_x == x, gathered[deep * x : deep * (x + 1)], air)
    air = air[:UL]
    onehot = (lax.broadcasted_iota(jnp.int32, (NCLS, slots), 0) == class_ref[...]).astype(jnp.float32)
    areas = dot(table[...], onehot, ((0,), (0,)))
    walls = wall_ref[...]
    indoor = indoor_ref[...]
    heat = heat_coef * areas * (walls[0:1] - air)
    wall_first = walls[0:1] - wall_coef * jnp.sum(heat, axis=0, keepdims=True) + conduct * (walls[1:2] - walls[0:1])
    middle = walls[1:-1] + conduct * (walls[:-2] - 2.0 * walls[1:-1] + walls[2:])
    last = walls[-1:] + conduct * (walls[-2:-1] - walls[-1:]) + inner_coef * (indoor - walls[-1:])
    indoor_new = indoor + room_coef * (walls[-1:] - indoor)
    live = lax.broadcasted_iota(jnp.int32, (1, slots), 1) < counts[0]
    wall_out[...] = jnp.where(live, jnp.concatenate([wall_first, middle, last], axis=0), walls)
    indoor_out[...] = jnp.where(live, indoor_new, indoor)
    heating = jnp.where(live, flux_coef * heat, 0.0)
    heating = jnp.concatenate([heating, jnp.zeros((deep - UL, slots), jnp.float32)], axis=0)
    spread = jnp.concatenate([jnp.where(cell_x == x, heating, 0.0) for x in range(x_size)], axis=0)
    added = dot(spread, at_y, ((1,), (1,)))
    for x in range(x_size):
        for t in range(deep // 8):
            out[pl.ds(8 * x_size * t + x, 8, stride=x_size), :] = (
                lower[x][8 * t : 8 * t + 8] + added[deep * x + 8 * t : deep * x + 8 * t + 8]
            )


def exchange(axis, low, high):
    size = lax.axis_size(axis)
    up = [(i, (i + 1) % size) for i in range(size)]
    down = [(j, i) for i, j in up]
    return lax.ppermute(high, axis, up), lax.ppermute(low, axis, down)


def per_device(
    scalars,
    winds,
    map_factor,
    urban_counts,
    urban_cols,
    street_class,
    area_table,
    wall_temp,
    indoor_temp,
):
    n_scalars, levels, x_size, y_size = scalars.shape
    slots = urban_cols.shape[0]
    rows = n_scalars * levels // CHUNKS
    f32 = functools.partial(jax.ShapeDtypeStruct, dtype=jnp.float32)
    field = scalars.reshape(n_scalars * levels * x_size, y_size)
    wind = winds.reshape(2 * levels * x_size, y_size)
    params = pltpu.CompilerParams(vmem_limit_bytes=40 * 2**20)
    whole = pl.BlockSpec(memory_space=pltpu.VMEM)

    lows, highs, packs = ([None] * CHUNKS for _ in range(3))
    for c in range(CHUNKS):
        extra = levels if c == 0 else 0
        lows[c], highs[c], packs[c] = pl.pallas_call(
            functools.partial(extract_kernel, None, x_size, c == 0),
            grid=(1,),
            in_specs=[pl.BlockSpec((rows * x_size, y_size), lambda g, c=c: (c, 0))] + [whole] * (c == 0),
            out_specs=[whole] * 3,
            out_shape=[
                f32((WIDTH * rows + extra, y_size)),
                f32((WIDTH * rows + extra, y_size)),
                f32((rows + extra, y_size)),
            ],
            compiler_params=params,
            name="extract",
        )(field, *([wind] if c == 0 else []))

    def swap(c):
        west, east = exchange("gx", lows[c], highs[c])
        south, north = exchange("gy", packs[c], packs[c])
        return west, east, south, north

    received = [swap(c) for c in range(CHUNKS)]
    west, east, south, north = received[0]
    edge_row = pl.BlockSpec((levels, y_size), lambda g: (WIDTH * rows // levels, 0))
    edge_pack = pl.BlockSpec((levels, y_size), lambda g: (rows // levels, 0))
    speeds = pl.pallas_call(
        functools.partial(wind_kernel, x_size),
        grid=(1,),
        in_specs=[whole, edge_row, edge_row, edge_pack, edge_pack, edge_pack],
        out_specs=[whole] * 3,
        out_shape=[f32((x_size + 1, levels, y_size)), f32((x_size, levels, y_size)), f32((levels, y_size))],
        compiler_params=params,
        name="speeds",
    )(wind, west, east, south, north, packs[0])

    block = levels
    steps = rows // block
    flat = pl.BlockSpec((block * x_size, y_size), lambda g: (g, 0))
    tall = pl.BlockSpec((x_size, block, y_size), lambda g: (0, g, 0))
    edge = pl.BlockSpec((WIDTH, block, y_size), lambda g: (0, g, 0))
    pack = pl.BlockSpec((block, y_size), lambda g: (g, 0))
    row_specs = [pl.BlockSpec((block, y_size), lambda g, j=j: (j * steps + g, 0)) for j in range(WIDTH)]
    flops = 3 * 45 * rows * x_size * y_size
    cost = pl.CostEstimate(flops=flops, bytes_accessed=16 * rows * x_size * y_size, transcendentals=0)
    sections = [None] * CHUNKS
    result = None
    for k, divisor in enumerate((3.0, 2.0, 1.0)):
        last = k == 2
        for c in range(CHUNKS):
            west, east, south, north = received[c]
            flat_c = pl.BlockSpec((block * x_size, y_size), lambda g, c=c: (c * steps + g, 0))
            operands = [field] if k == 0 else [sections[c], field]
            specs = [flat_c] if k == 0 else [tall, flat_c]
            operands += [west.reshape(-1, y_size)] * 3 + [east.reshape(-1, y_size)] * 3
            specs += row_specs * 2
            operands += [south, north, packs[c], *speeds, map_factor]
            specs += [pack] * 3 + [whole] * 4
            city = last and c == 0
            aliases = {}
            if city:
                operands += [
                    urban_counts,
                    urban_cols[None],
                    street_class[None],
                    area_table,
                    wall_temp,
                    indoor_temp[None],
                ]
                specs += [pl.BlockSpec(memory_space=pltpu.SMEM)] + [whole] * 5
                out_specs = [flat_c, whole, whole]
                out_shape = [f32(field.shape), f32(wall_temp.shape), f32((1, slots))]
            elif last:
                aliases = {len(operands): 0}
                operands += [result]
                specs += [pl.BlockSpec(memory_space=pl.ANY)]
                out_specs = [flat_c]
                out_shape = [f32(field.shape)]
            else:
                out_specs = [tall, edge, edge, pack]
                out_shape = [
                    f32((x_size, rows, y_size)),
                    f32((WIDTH, rows, y_size)),
                    f32((WIDTH, rows, y_size)),
                    f32((rows, y_size)),
                ]
            outs = pl.pallas_call(
                functools.partial(section_kernel, x_size, divisor, k == 0, last, city),
                grid=(steps,),
                in_specs=specs,
                out_specs=out_specs,
                out_shape=out_shape,
                input_output_aliases=aliases,
                compiler_params=params,
                cost_estimate=cost,
                name=f"section_{k}_{c}",
            )(*operands)
            if city:
                result, wall_out, indoor_out = outs
            elif last:
                (result,) = outs
            else:
                sections[c], lows[c], highs[c], packs[c] = outs
                received[c] = swap(c)
    return (result.reshape(scalars.shape), wall_out, indoor_out[0])


def solution(mesh):
    in_specs = (
        P(None, None, "gx", "gy"),
        P(None, None, "gx", "gy"),
        P("gx", "gy"),
        P(("gx", "gy")),
        P(("gx", "gy")),
        P(("gx", "gy")),
        P(),
        P(None, ("gx", "gy")),
        P(("gx", "gy")),
    )
    out_specs = (P(None, None, "gx", "gy"), P(None, ("gx", "gy")), P(("gx", "gy")))
    return jax.shard_map(
        per_device, mesh=mesh, in_specs=in_specs, out_specs=out_specs, check_vma=False
    )
```

```python
import functools

import jax
import jax.numpy as jnp
import ml_dtypes
import numpy as np
from jax import lax
from jax.experimental import pallas as pl
from jax.experimental.pallas import tpu as pltpu
from jax.sharding import PartitionSpec as P

UL = 10
NWL = 10
NCLS = 10
WIDTH = 3
GROUP = 8
CHUNKS = 2
PIECE = 256
DIVISORS = (3.0, 2.0, 1.0)
HIGH = (1, -8, 37, 37, -8, 1)
DAMP = (-1, 5, -10, 10, -5, 1)

heat_coef = 0.5
wall_coef = 0.05
conduct = 0.3
inner_coef = 0.2
room_coef = 0.1
flux_coef = 0.5
face_scale = 0.5 / 60.0


def lane_index(shape):
    return lax.broadcasted_iota(jnp.int32, shape, 1)


def rolled(array, shift):
    return pltpu.roll(array, shift % array.shape[1], 1)


def pack_edges(packed, row, x):
    moved = rolled(row, GROUP * x + WIDTH)
    lane = lane_index(row.shape)
    here = (lane >= GROUP * x) & (lane < GROUP * x + 2 * WIDTH)
    return moved if packed is None else jnp.where(here, moved, packed)


def ahead(row, halo, lane, k):
    if k > 0:
        return rolled(jnp.where(lane < k, halo, row), -k)
    return rolled(jnp.where(lane >= row.shape[1] + k, halo, row), -k)


def extract_kernel(tiles, x_size, with_wind, *refs):
    if with_wind:
        field, wind, low, high, packed = refs
    else:
        field, low, high, packed = refs
    rows = field.shape[0] // x_size

    def one(t, carry):
        base = pl.multiple_of(t * 8 * x_size, 8 * x_size)
        edges = None
        for x in range(x_size):
            row = field[pl.ds(base + x, 8, stride=x_size), :]
            if x < WIDTH:
                low[pl.ds(pl.multiple_of(x * rows + t * 8, 8), 8), :] = row
            if x >= x_size - WIDTH:
                at = (x - x_size + WIDTH) * rows
                high[pl.ds(pl.multiple_of(at + t * 8, 8), 8), :] = row
            edges = pack_edges(edges, row, x)
        packed[pl.ds(pl.multiple_of(t * 8, 8), 8), :] = edges
        return carry

    lax.fori_loop(0, rows // 8, one, 0)
    if with_wind:
        levels = wind.shape[0] // (2 * x_size)

        def one_wind(t, carry):
            base = pl.multiple_of(t * 8 * x_size, 8 * x_size)
            at = pl.ds(pl.multiple_of(WIDTH * rows + t * 8, 8), 8)
            low[at, :] = wind[pl.ds(base, 8, stride=x_size), :]
            high[at, :] = wind[pl.ds(base + x_size - 1, 8, stride=x_size), :]
            base = base + levels * x_size
            edges = None
            for x in range(x_size):
                edges = pack_edges(edges, wind[pl.ds(base + x, 8, stride=x_size), :], x)
            packed[pl.ds(pl.multiple_of(rows + t * 8, 8), 8), :] = edges
            return carry

        lax.fori_loop(0, levels // 8, one_wind, 0)


def wind_kernel(x_size, wind, factor, west, east, south, north, speed_x, ahead_y, behind_y, edge_ahead, edge_behind, scales):
    levels = speed_x.shape[1]
    for x in range(x_size):
        mapped = factor[pl.ds(x, 1), :]
        for k, divisor in enumerate(DIVISORS):
            scales[k, x] = jnp.broadcast_to(mapped * mapped * (-1.0 / divisor), scales.shape[2:])

    def one(t, carry):
        base = pl.multiple_of(t * 8 * x_size, 8 * x_size)
        at = pl.ds(pl.multiple_of(t * 8, 8), 8)
        before = west[at, :]
        for x in range(x_size + 1):
            now = east[at, :] if x == x_size else wind[pl.ds(base + x, 8, stride=x_size), :]
            speed_x[x, at, :] = face_scale * (before + now)
            before = now
        base = base + levels * x_size
        lane = lane_index(before.shape)
        first = (lane & (GROUP - 1)) < WIDTH
        halo = jnp.where(first, south[at, :], north[at, :])
        forward, backward = None, None
        for x in range(x_size):
            row = wind[pl.ds(base + x, 8, stride=x_size), :]
            edge = rolled(halo, -(GROUP * x + WIDTH))
            front = face_scale * (row + ahead(row, edge, lane, 1))
            back = face_scale * (row + ahead(row, edge, lane, -1))
            ahead_y[x, at, :] = front
            behind_y[x, at, :] = back
            forward = pack_edges(forward, front, x)
            backward = pack_edges(backward, back, x)
        edge_ahead[at, :] = forward
        edge_behind[at, :] = backward
        return carry

    lax.fori_loop(0, levels // 8, one, 0)


def stencil_matrices(y_size):
    inner = np.zeros((y_size, 4 * y_size), np.float32)
    edges = np.zeros((y_size, 4 * y_size), np.float32)
    for part, (taps, offset) in enumerate(((HIGH, -2), (DAMP, -2), (HIGH, -3), (DAMP, -3))):
        for n, tap in enumerate(taps):
            k = n + offset
            for j in range(y_size):
                if 0 <= j + k < y_size:
                    inner[j + k, part * y_size + j] = tap
            for g in range(0, y_size, GROUP):
                for j in range(WIDTH):
                    if j + k < 0:
                        edges[g + WIDTH + j + k, part * y_size + g + WIDTH + j] = tap
                    if j - WIDTH + k >= 0:
                        edges[g + j + k, part * y_size + g + j] = tap
    return [jnp.asarray(np.concatenate([m, m]).astype(ml_dtypes.bfloat16)) for m in (inner, edges)]


def stencil_product(values, matrix):
    leading = values.astype(jnp.bfloat16)
    trailing = (values - leading.astype(jnp.float32)).astype(jnp.bfloat16)
    return jnp.dot(
        jnp.concatenate([leading, trailing], axis=1), matrix[...], preferred_element_type=jnp.float32
    )


def section_kernel(x_size, k, last, with_city, *refs):
    refs = list(refs)
    first = k == 0
    section = refs.pop(0)
    base_ref = section if first else refs.pop(0)
    west = [refs.pop(0) for _ in range(WIDTH)]
    east = [refs.pop(0) for _ in range(WIDTH)]
    south, north = [refs.pop(0) for _ in range(2)]
    speed_x, ahead_y, behind_y, edge_ahead, edge_behind, scales = [refs.pop(0) for _ in range(6)]
    inner_matrix, edge_matrix = [refs.pop(0) for _ in range(2)]
    parts = refs[-4:]
    share = refs[-5]
    refs = refs[:-5]
    rows, y_size = south.shape
    if last:
        if with_city:
            city = [refs.pop(0) for _ in range(6)]
            out, wall_out, indoor_out = refs
        else:
            refs.pop(0)
            (out,) = refs
    else:
        out, low, high, packed = refs

    total = rows * x_size
    piece = PIECE
    for p in range(total // piece):
        if first:
            values = section[p * piece : (p + 1) * piece, :]
        else:
            n = piece // rows
            values = section[p * n : (p + 1) * n].reshape(piece, y_size)
        product = stencil_product(values, inner_matrix)
        for j, part in enumerate(parts):
            part[p * piece : (p + 1) * piece, :] = product[:, j * y_size : (j + 1) * y_size]
    lane = lane_index((rows, y_size))
    halo = jnp.where((lane & (GROUP - 1)) < WIDTH, south[...], north[...])
    product = stencil_product(halo, edge_matrix)
    after, before = edge_ahead[...], edge_behind[...]
    share[...] = (
        after * product[:, :y_size]
        - jnp.abs(after) * product[:, y_size : 2 * y_size]
        - before * product[:, 2 * y_size : 3 * y_size]
        + jnp.abs(before) * product[:, 3 * y_size :]
    )

    def one(t, carry):
        at = pl.ds(pl.multiple_of(t * 8, 8), 8)
        start = pl.multiple_of(t * 8 * x_size, 8 * x_size)

        def across(ref, x):
            return ref[pl.ds(start + x, 8, stride=x_size), :]

        def cell(x):
            if x < 0:
                return west[x + WIDTH][at, :]
            if x >= x_size:
                return east[x - x_size][at, :]
            return across(section, x) if first else section[x, at, :]

        lane = lane_index((8, y_size))
        edge_lane = (lane < WIDTH) | (lane >= y_size - WIDTH)
        edge_share = share[at, :]
        q = [cell(x) for x in range(-3, 2)]
        d1 = [q[i + 1] - q[i] for i in range(4)]
        d2 = [d1[i + 1] - d1[i] for i in range(3)]
        d3 = [d2[i + 1] - d2[i] for i in range(2)]
        d4 = d3[1] - d3[0]
        smooth = d4 - 5.0 * d2[1] + 30.0 * q[2]
        q, d1, d2, d3 = q[3:], d1[-1], d2[-1], d3[-1]
        flux_before = None
        edges = None
        for x in range(-1, x_size):
            q.append(cell(x + WIDTH))
            new1 = q[-1] - q[-2]
            new2 = new1 - d1
            new3 = new2 - d2
            new4 = new3 - d3
            new_smooth = new4 - 5.0 * d2 + 30.0 * q[0]
            speed = speed_x[x + 1, at, :]
            flux = speed * (smooth + new_smooth) - jnp.abs(speed) * (new4 - d4)
            d1, d2, d3, d4, smooth = new1, new2, new3, new4, new_smooth
            if x >= 0:
                if first:
                    lines = [across(part, x) for part in parts]
                else:
                    lines = [part[pl.ds(pl.multiple_of(x * rows + t * 8, 8), 8), :] for part in parts]
                after, before = ahead_y[x, at, :], behind_y[x, at, :]
                moved = rolled(edge_share, -(GROUP * x + WIDTH))
                divergence = (
                    (flux - flux_before)
                    + (after * lines[0] - jnp.abs(after) * lines[1])
                    - (before * lines[2] - jnp.abs(before) * lines[3])
                    + jnp.where(edge_lane, moved, 0.0)
                )
                new = across(base_ref, x) + scales[k, x] * divergence
                if last:
                    out[pl.ds(start + x, 8, stride=x_size), :] = new
                else:
                    out[x, at, :] = new
                    if x < WIDTH:
                        low[x, at, :] = new
                    if x >= x_size - WIDTH:
                        high[x - x_size + WIDTH, at, :] = new
                    edges = pack_edges(edges, new, x)
            flux_before = flux
            q = q[1:]
        if not last:
            packed[at, :] = edges
        return carry

    lax.fori_loop(0, rows // 8, one, 0)
    if last and with_city:

        @pl.when(pl.program_id(0) == 0)
        def _():
            city_step(x_size, out, *city, wall_out, indoor_out)


def dot(a, b, dims):
    return lax.dot_general(
        a, b, (dims, ((), ())), precision=lax.Precision.HIGHEST, preferred_element_type=jnp.float32
    )


def city_step(x_size, out, counts, cols_ref, class_ref, table, wall_ref, indoor_ref, wall_out, indoor_out):
    deep = 16
    cols = cols_ref[...]
    slots = cols.shape[1]
    y_size = out.shape[1]
    cell_x = lax.div(cols, y_size)
    cell_y = lax.rem(cols, y_size)
    lower = [
        jnp.concatenate([out[pl.ds(8 * x_size * t + x, 8, stride=x_size), :] for t in range(deep // 8)], axis=0)
        for x in range(x_size)
    ]
    at_y = (lax.broadcasted_iota(jnp.int32, (y_size, slots), 0) == cell_y).astype(jnp.float32)
    gathered = dot(jnp.concatenate(lower, axis=0), at_y, ((1,), (0,)))
    air = jnp.zeros((deep, slots), jnp.float32)
    for x in range(x_size):
        air = jnp.where(cell_x == x, gathered[deep * x : deep * (x + 1)], air)
    air = air[:UL]
    onehot = (lax.broadcasted_iota(jnp.int32, (NCLS, slots), 0) == class_ref[...]).astype(jnp.float32)
    areas = dot(table[...], onehot, ((0,), (0,)))
    walls = wall_ref[...]
    indoor = indoor_ref[...]
    heat = heat_coef * areas * (walls[0:1] - air)
    wall_first = walls[0:1] - wall_coef * jnp.sum(heat, axis=0, keepdims=True) + conduct * (walls[1:2] - walls[0:1])
    middle = walls[1:-1] + conduct * (walls[:-2] - 2.0 * walls[1:-1] + walls[2:])
    last = walls[-1:] + conduct * (walls[-2:-1] - walls[-1:]) + inner_coef * (indoor - walls[-1:])
    indoor_new = indoor + room_coef * (walls[-1:] - indoor)
    live = lax.broadcasted_iota(jnp.int32, (1, slots), 1) < counts[0]
    wall_out[...] = jnp.where(live, jnp.concatenate([wall_first, middle, last], axis=0), walls)
    indoor_out[...] = jnp.where(live, indoor_new, indoor)
    heating = jnp.where(live, flux_coef * heat, 0.0)
    heating = jnp.concatenate([heating, jnp.zeros((deep - UL, slots), jnp.float32)], axis=0)
    spread = jnp.concatenate([jnp.where(cell_x == x, heating, 0.0) for x in range(x_size)], axis=0)
    added = dot(spread, at_y, ((1,), (1,)))
    for x in range(x_size):
        for t in range(deep // 8):
            out[pl.ds(8 * x_size * t + x, 8, stride=x_size), :] = (
                lower[x][8 * t : 8 * t + 8] + added[deep * x + 8 * t : deep * x + 8 * t + 8]
            )


def exchange(axis, low, high):
    size = lax.axis_size(axis)
    up = [(i, (i + 1) % size) for i in range(size)]
    down = [(j, i) for i, j in up]
    return lax.ppermute(high, axis, up), lax.ppermute(low, axis, down)


def per_device(
    scalars,
    winds,
    map_factor,
    urban_counts,
    urban_cols,
    street_class,
    area_table,
    wall_temp,
    indoor_temp,
):
    n_scalars, levels, x_size, y_size = scalars.shape
    slots = urban_cols.shape[0]
    rows = n_scalars * levels // CHUNKS
    f32 = functools.partial(jax.ShapeDtypeStruct, dtype=jnp.float32)
    field = scalars.reshape(n_scalars * levels * x_size, y_size)
    wind = winds.reshape(2 * levels * x_size, y_size)
    params = pltpu.CompilerParams(vmem_limit_bytes=40 * 2**20)
    whole = pl.BlockSpec(memory_space=pltpu.VMEM)

    lows, highs, packs = ([None] * CHUNKS for _ in range(3))
    for c in range(CHUNKS):
        extra = levels if c == 0 else 0
        lows[c], highs[c], packs[c] = pl.pallas_call(
            functools.partial(extract_kernel, None, x_size, c == 0),
            grid=(1,),
            in_specs=[pl.BlockSpec((rows * x_size, y_size), lambda g, c=c: (c, 0))] + [whole] * (c == 0),
            out_specs=[whole] * 3,
            out_shape=[
                f32((WIDTH * rows + extra, y_size)),
                f32((WIDTH * rows + extra, y_size)),
                f32((rows + extra, y_size)),
            ],
            compiler_params=params,
            name="extract",
        )(field, *([wind] if c == 0 else []))

    def swap(c):
        west, east = exchange("gx", lows[c], highs[c])
        south, north = exchange("gy", packs[c], packs[c])
        return west, east, south, north

    received = [swap(c) for c in range(CHUNKS)]
    west, east, south, north = received[0]
    edge_row = pl.BlockSpec((levels, y_size), lambda g: (WIDTH * rows // levels, 0))
    edge_pack = pl.BlockSpec((levels, y_size), lambda g: (rows // levels, 0))
    speeds = pl.pallas_call(
        functools.partial(wind_kernel, x_size),
        grid=(1,),
        in_specs=[whole, whole, edge_row, edge_row, edge_pack, edge_pack],
        out_specs=[whole] * 6,
        out_shape=[
            f32((x_size + 1, levels, y_size)),
            f32((x_size, levels, y_size)),
            f32((x_size, levels, y_size)),
            f32((levels, y_size)),
            f32((levels, y_size)),
            f32((len(DIVISORS), x_size, 8, y_size)),
        ],
        compiler_params=params,
        name="speeds",
    )(wind, map_factor, west, east, south, north)
    matrices = stencil_matrices(y_size)

    block = levels
    steps = rows // block
    flat = pl.BlockSpec((block * x_size, y_size), lambda g: (g, 0))
    tall = pl.BlockSpec((x_size, block, y_size), lambda g: (0, g, 0))
    edge = pl.BlockSpec((WIDTH, block, y_size), lambda g: (0, g, 0))
    pack = pl.BlockSpec((block, y_size), lambda g: (g, 0))
    row_specs = [pl.BlockSpec((block, y_size), lambda g, j=j: (j * steps + g, 0)) for j in range(WIDTH)]
    flops = 3 * 45 * rows * x_size * y_size
    cost = pl.CostEstimate(flops=flops, bytes_accessed=16 * rows * x_size * y_size, transcendentals=0)
    sections = [None] * CHUNKS
    result = None
    for k in range(len(DIVISORS)):
        last = k == len(DIVISORS) - 1
        for c in range(CHUNKS):
            west, east, south, north = received[c]
            flat_c = pl.BlockSpec((block * x_size, y_size), lambda g, c=c: (c * steps + g, 0))
            operands = [field] if k == 0 else [sections[c], field]
            specs = [flat_c] if k == 0 else [tall, flat_c]
            operands += [west.reshape(-1, y_size)] * 3 + [east.reshape(-1, y_size)] * 3
            specs += row_specs * 2
            operands += [south, north, *speeds, *matrices]
            specs += [pack] * 2 + [whole] * 8
            city = last and c == 0
            aliases = {}
            if city:
                operands += [
                    urban_counts,
                    urban_cols[None],
                    street_class[None],
                    area_table,
                    wall_temp,
                    indoor_temp[None],
                ]
                specs += [pl.BlockSpec(memory_space=pltpu.SMEM)] + [whole] * 5
                out_specs = [flat_c, whole, whole]
                out_shape = [f32(field.shape), f32(wall_temp.shape), f32((1, slots))]
            elif last:
                aliases = {len(operands): 0}
                operands += [result]
                specs += [pl.BlockSpec(memory_space=pl.ANY)]
                out_specs = [flat_c]
                out_shape = [f32(field.shape)]
            else:
                out_specs = [tall, edge, edge, pack]
                out_shape = [
                    f32((x_size, rows, y_size)),
                    f32((WIDTH, rows, y_size)),
                    f32((WIDTH, rows, y_size)),
                    f32((rows, y_size)),
                ]
            outs = pl.pallas_call(
                functools.partial(section_kernel, x_size, k, last, city),
                grid=(steps,),
                in_specs=specs,
                out_specs=out_specs,
                out_shape=out_shape,
                scratch_shapes=[pltpu.VMEM((block, y_size), jnp.float32)]
                + [pltpu.VMEM((block * x_size, y_size), jnp.float32)] * 4,
                input_output_aliases=aliases,
                compiler_params=params,
                cost_estimate=cost,
                name=f"section_{k}_{c}",
            )(*operands)
            if city:
                result, wall_out, indoor_out = outs
            elif last:
                (result,) = outs
            else:
                sections[c], lows[c], highs[c], packs[c] = outs
                received[c] = swap(c)
    return (result.reshape(scalars.shape), wall_out, indoor_out[0])


def solution(mesh):
    in_specs = (
        P(None, None, "gx", "gy"),
        P(None, None, "gx", "gy"),
        P("gx", "gy"),
        P(("gx", "gy")),
        P(("gx", "gy")),
        P(("gx", "gy")),
        P(),
        P(None, ("gx", "gy")),
        P(("gx", "gy")),
    )
    out_specs = (P(None, None, "gx", "gy"), P(None, ("gx", "gy")), P(("gx", "gy")))
    return jax.shard_map(
        per_device, mesh=mesh, in_specs=in_specs, out_specs=out_specs, check_vma=False
    )
```

```python
import functools

import jax
import jax.numpy as jnp
import ml_dtypes
import numpy as np
from jax import lax
from jax.experimental import pallas as pl
from jax.experimental.pallas import tpu as pltpu
from jax.sharding import PartitionSpec as P

UL = 10
NWL = 10
NCLS = 10
WIDTH = 3
GROUP = 8
CHUNKS = 2
PIECE = 256
DIVISORS = (3.0, 2.0, 1.0)
HIGH = (1, -8, 37, 37, -8, 1)
DAMP = (-1, 5, -10, 10, -5, 1)

heat_coef = 0.5
wall_coef = 0.05
conduct = 0.3
inner_coef = 0.2
room_coef = 0.1
flux_coef = 0.5
face_scale = 0.5 / 60.0


def lane_index(shape):
    return lax.broadcasted_iota(jnp.int32, shape, 1)


def rolled(array, shift):
    return pltpu.roll(array, shift % array.shape[1], 1)


def pack_edges(packed, row, x):
    moved = rolled(row, GROUP * x + WIDTH)
    lane = lane_index(row.shape)
    here = (lane >= GROUP * x) & (lane < GROUP * x + 2 * WIDTH)
    return moved if packed is None else jnp.where(here, moved, packed)


def ahead(row, halo, lane, k):
    if k > 0:
        return rolled(jnp.where(lane < k, halo, row), -k)
    return rolled(jnp.where(lane >= row.shape[1] + k, halo, row), -k)


def first_rows_kernel(x_size, rows, levels, pieces, odd, field, wind, to_a, to_b, field_here, wind_here, sems):
    size = rows * x_size // pieces
    copies = [
        pltpu.make_async_copy(field.at[pl.ds(p * size, size), :], field_here.at[pl.ds(p * size, size), :], sems.at[p])
        for p in range(pieces)
    ]
    copies.append(pltpu.make_async_copy(wind.at[pl.ds(0, levels * x_size), :], wind_here, sems.at[pieces]))
    for copy in copies:
        copy.start()
    even = odd[0] == 0
    for p in range(pieces):
        copies[p].wait()
        for t in range(p * rows // pieces // 8, (p + 1) * rows // pieces // 8):
            for j in range(WIDTH):
                low = field_here[pl.ds(t * 8 * x_size + j, 8, stride=x_size), :]
                high = field_here[pl.ds(t * 8 * x_size + x_size - WIDTH + j, 8, stride=x_size), :]
                to_a[j * rows + t * 8 : j * rows + t * 8 + 8, :] = jnp.where(even, high, low)
                to_b[j * rows + t * 8 : j * rows + t * 8 + 8, :] = jnp.where(even, low, high)
    copies[pieces].wait()
    for t in range(levels // 8):
        low = wind_here[pl.ds(t * 8 * x_size, 8, stride=x_size), :]
        high = wind_here[pl.ds(t * 8 * x_size + x_size - 1, 8, stride=x_size), :]
        at = WIDTH * rows + t * 8
        to_a[at : at + 8, :] = jnp.where(even, high, low)
        to_b[at : at + 8, :] = jnp.where(even, low, high)


def extract_kernel(x_size, chunk, with_wind, odd, field, *refs):
    if with_wind:
        wind, packed = refs
    else:
        to_a, to_b, packed = refs
    rows = packed.shape[0]
    if with_wind:
        levels = wind.shape[0] // (2 * x_size)
        rows = rows - levels
    even = odd[0] == 0

    def one(t, carry):
        base = pl.multiple_of((chunk * rows + t * 8) * x_size, 8 * x_size)
        edges = None
        for x in range(x_size):
            edges = pack_edges(edges, field[pl.ds(base + x, 8, stride=x_size), :], x)
        packed[pl.ds(pl.multiple_of(t * 8, 8), 8), :] = edges
        if not with_wind:
            for j in range(WIDTH):
                low = field[pl.ds(base + j, 8, stride=x_size), :]
                high = field[pl.ds(base + x_size - WIDTH + j, 8, stride=x_size), :]
                at = pl.ds(pl.multiple_of(j * rows + t * 8, 8), 8)
                to_a[at, :] = jnp.where(even, high, low)
                to_b[at, :] = jnp.where(even, low, high)
        return carry

    lax.fori_loop(0, rows // 8, one, 0)
    if with_wind:

        def one_wind(t, carry):
            base = pl.multiple_of((levels + t * 8) * x_size, 8 * x_size)
            edges = None
            for x in range(x_size):
                edges = pack_edges(edges, wind[pl.ds(base + x, 8, stride=x_size), :], x)
            packed[pl.ds(pl.multiple_of(rows + t * 8, 8), 8), :] = edges
            return carry

        lax.fori_loop(0, levels // 8, one_wind, 0)


def join_packs(even, from_a, from_b):
    south = jnp.where(even, from_b, from_a)
    north = jnp.where(even, from_a, from_b)
    return jnp.where((lane_index(south.shape) & (GROUP - 1)) < WIDTH, south, north)


def wind_kernel(x_size, rows, odd, wind, factor, from_a, from_b, pack_a, pack_b, *outs):
    speed_x, ahead_y, behind_y, edge_ahead, edge_behind, scales = outs
    levels = speed_x.shape[1]
    even_x, even_y = odd[0] == 0, odd[1] == 0
    for x in range(x_size):
        mapped = factor[pl.ds(x, 1), :]
        for k, divisor in enumerate(DIVISORS):
            scales[k, x] = jnp.broadcast_to(mapped * mapped * (-1.0 / divisor), scales.shape[2:])

    def one(t, carry):
        base = pl.multiple_of(t * 8 * x_size, 8 * x_size)
        at = pl.ds(pl.multiple_of(t * 8, 8), 8)
        there = pl.ds(pl.multiple_of(WIDTH * rows + t * 8, 8), 8)
        before = jnp.where(even_x, from_b[there, :], from_a[there, :])
        east = jnp.where(even_x, from_a[there, :], from_b[there, :])
        for x in range(x_size + 1):
            now = east if x == x_size else wind[pl.ds(base + x, 8, stride=x_size), :]
            speed_x[x, at, :] = face_scale * (before + now)
            before = now
        base = base + levels * x_size
        lane = lane_index(before.shape)
        there = pl.ds(pl.multiple_of(rows + t * 8, 8), 8)
        halo = join_packs(even_y, pack_a[there, :], pack_b[there, :])
        forward, backward = None, None
        for x in range(x_size):
            row = wind[pl.ds(base + x, 8, stride=x_size), :]
            edge = rolled(halo, -(GROUP * x + WIDTH))
            front = face_scale * (row + ahead(row, edge, lane, 1))
            back = face_scale * (row + ahead(row, edge, lane, -1))
            ahead_y[x, at, :] = front
            behind_y[x, at, :] = back
            forward = pack_edges(forward, front, x)
            backward = pack_edges(backward, back, x)
        edge_ahead[at, :] = forward
        edge_behind[at, :] = backward
        return carry

    lax.fori_loop(0, levels // 8, one, 0)


def stencil_matrices(y_size):
    inner = np.zeros((y_size, 4 * y_size), np.float32)
    edges = np.zeros((y_size, 4 * y_size), np.float32)
    for part, (taps, offset) in enumerate(((HIGH, -2), (DAMP, -2), (HIGH, -3), (DAMP, -3))):
        for n, tap in enumerate(taps):
            k = n + offset
            for j in range(y_size):
                if 0 <= j + k < y_size:
                    inner[j + k, part * y_size + j] = tap
            for g in range(0, y_size, GROUP):
                for j in range(WIDTH):
                    if j + k < 0:
                        edges[g + WIDTH + j + k, part * y_size + g + WIDTH + j] = tap
                    if j - WIDTH + k >= 0:
                        edges[g + j + k, part * y_size + g + j] = tap
    return [jnp.asarray(np.concatenate([m, m]).astype(ml_dtypes.bfloat16)) for m in (inner, edges)]


def stencil_product(values, matrix):
    leading = values.astype(jnp.bfloat16)
    trailing = (values - leading.astype(jnp.float32)).astype(jnp.bfloat16)
    return jnp.dot(
        jnp.concatenate([leading, trailing], axis=1), matrix[...], preferred_element_type=jnp.float32
    )


def section_kernel(x_size, k, chunk, last, with_city, odd, *refs):
    refs = list(refs)
    first = k == 0
    section = refs.pop(0)
    base_ref = section if first else refs.pop(0)
    from_a, from_b, pack_a, pack_b = [refs.pop(0) for _ in range(4)]
    speed_x, ahead_y, behind_y, edge_ahead, edge_behind, scales = [refs.pop(0) for _ in range(6)]
    inner_matrix, edge_matrix = [refs.pop(0) for _ in range(2)]
    parts = refs[-4:]
    share = refs[-5]
    refs = refs[:-5]
    if last:
        if with_city:
            city = [refs.pop(0) for _ in range(6)]
            out, wall_out, indoor_out = refs
        else:
            refs.pop(0)
            (out,) = refs
    else:
        out, to_a, to_b, packed = refs
    levels, y_size = edge_ahead.shape
    chunk_rows = base_ref.shape[0] // (CHUNKS * x_size)
    even_x, even_y = odd[0] == 0, odd[1] == 0

    def block(g, carry):
        corner = pl.multiple_of((chunk * chunk_rows + g * levels) * x_size, levels * x_size)
        here = pl.multiple_of(g * levels, levels)
        for p in range(levels * x_size // PIECE):
            if first:
                values = section[pl.ds(pl.multiple_of(corner + p * PIECE, PIECE), PIECE), :]
            else:
                n = PIECE // levels
                values = section[p * n : (p + 1) * n, pl.ds(here, levels), :].reshape(PIECE, y_size)
            product = stencil_product(values, inner_matrix)
            for j, part in enumerate(parts):
                part[p * PIECE : (p + 1) * PIECE, :] = product[:, j * y_size : (j + 1) * y_size]
        halo = join_packs(even_y, pack_a[pl.ds(here, levels), :], pack_b[pl.ds(here, levels), :])
        product = stencil_product(halo, edge_matrix)
        after, before = edge_ahead[...], edge_behind[...]
        share[...] = (
            after * product[:, :y_size]
            - jnp.abs(after) * product[:, y_size : 2 * y_size]
            - before * product[:, 2 * y_size : 3 * y_size]
            + jnp.abs(before) * product[:, 3 * y_size :]
        )

        def one(t, carry):
            at = pl.ds(pl.multiple_of(t * 8, 8), 8)
            rows_at = pl.ds(pl.multiple_of(here + t * 8, 8), 8)
            start = pl.multiple_of(corner + t * 8 * x_size, 8 * x_size)

            def halo_rows(mine, other, j):
                edge_at = pl.ds(pl.multiple_of(j * chunk_rows + here + t * 8, 8), 8)
                return jnp.where(even_x, mine[edge_at, :], other[edge_at, :])

            def cell(x):
                if x < 0:
                    return halo_rows(from_b, from_a, x + WIDTH)
                if x >= x_size:
                    return halo_rows(from_a, from_b, x - x_size)
                return section[pl.ds(start + x, 8, stride=x_size), :] if first else section[x, rows_at, :]

            lane = lane_index((8, y_size))
            edge_lane = (lane < WIDTH) | (lane >= y_size - WIDTH)
            edge_share = share[at, :]
            q = [cell(x) for x in range(-3, 2)]
            d1 = [q[i + 1] - q[i] for i in range(4)]
            d2 = [d1[i + 1] - d1[i] for i in range(3)]
            d3 = [d2[i + 1] - d2[i] for i in range(2)]
            d4 = d3[1] - d3[0]
            smooth = d4 - 5.0 * d2[1] + 30.0 * q[2]
            q, d1, d2, d3 = q[3:], d1[-1], d2[-1], d3[-1]
            flux_before = None
            edges = None
            for x in range(-1, x_size):
                q.append(cell(x + WIDTH))
                new1 = q[-1] - q[-2]
                new2 = new1 - d1
                new3 = new2 - d2
                new4 = new3 - d3
                new_smooth = new4 - 5.0 * d2 + 30.0 * q[0]
                speed = speed_x[x + 1, at, :]
                flux = speed * (smooth + new_smooth) - jnp.abs(speed) * (new4 - d4)
                d1, d2, d3, d4, smooth = new1, new2, new3, new4, new_smooth
                if x >= 0:
                    if first:
                        lines = [part[pl.ds(t * 8 * x_size + x, 8, stride=x_size), :] for part in parts]
                    else:
                        lines = [part[pl.ds(pl.multiple_of(x * levels + t * 8, 8), 8), :] for part in parts]
                    after, before = ahead_y[x, at, :], behind_y[x, at, :]
                    moved = rolled(edge_share, -(GROUP * x + WIDTH))
                    divergence = (
                        (flux - flux_before)
                        + (after * lines[0] - jnp.abs(after) * lines[1])
                        - (before * lines[2] - jnp.abs(before) * lines[3])
                        + jnp.where(edge_lane, moved, 0.0)
                    )
                    base = base_ref[pl.ds(start + x, 8, stride=x_size), :]
                    new = base + scales[k, x] * divergence
                    if last:
                        out[pl.ds(pl.multiple_of(t * 8 * x_size, 8 * x_size) + x, 8, stride=x_size), :] = new
                    else:
                        out[x, rows_at, :] = new
                        edges = pack_edges(edges, new, x)
                flux_before = flux
                q = q[1:]
            if not last:
                packed[rows_at, :] = edges
                for j in range(WIDTH):
                    low, high = out[j, rows_at, :], out[x_size - WIDTH + j, rows_at, :]
                    edge_at = pl.ds(pl.multiple_of(j * chunk_rows + here + t * 8, 8), 8)
                    to_a[edge_at, :] = jnp.where(even_x, high, low)
                    to_b[edge_at, :] = jnp.where(even_x, low, high)
            return carry

        lax.fori_loop(0, levels // 8, one, 0)
        return carry

    if last:
        block(pl.program_id(0), 0)
    else:
        lax.fori_loop(0, chunk_rows // levels, block, 0)
    if last and with_city:

        @pl.when(pl.program_id(0) == 0)
        def _():
            city_step(x_size, out, *city, wall_out, indoor_out)


def dot(a, b, dims):
    return lax.dot_general(
        a, b, (dims, ((), ())), precision=lax.Precision.HIGHEST, preferred_element_type=jnp.float32
    )


def city_step(x_size, out, counts, cols_ref, class_ref, table, wall_ref, indoor_ref, wall_out, indoor_out):
    deep = 16
    cols = cols_ref[...]
    slots = cols.shape[1]
    y_size = out.shape[1]
    cell_x = lax.div(cols, y_size)
    cell_y = lax.rem(cols, y_size)
    lower = [
        jnp.concatenate([out[pl.ds(8 * x_size * t + x, 8, stride=x_size), :] for t in range(deep // 8)], axis=0)
        for x in range(x_size)
    ]
    at_y = (lax.broadcasted_iota(jnp.int32, (y_size, slots), 0) == cell_y).astype(jnp.float32)
    gathered = dot(jnp.concatenate(lower, axis=0), at_y, ((1,), (0,)))
    air = jnp.zeros((deep, slots), jnp.float32)
    for x in range(x_size):
        air = jnp.where(cell_x == x, gathered[deep * x : deep * (x + 1)], air)
    air = air[:UL]
    onehot = (lax.broadcasted_iota(jnp.int32, (NCLS, slots), 0) == class_ref[...]).astype(jnp.float32)
    areas = dot(table[...], onehot, ((0,), (0,)))
    walls = wall_ref[...]
    indoor = indoor_ref[...]
    heat = heat_coef * areas * (walls[0:1] - air)
    wall_first = walls[0:1] - wall_coef * jnp.sum(heat, axis=0, keepdims=True) + conduct * (walls[1:2] - walls[0:1])
    middle = walls[1:-1] + conduct * (walls[:-2] - 2.0 * walls[1:-1] + walls[2:])
    last = walls[-1:] + conduct * (walls[-2:-1] - walls[-1:]) + inner_coef * (indoor - walls[-1:])
    indoor_new = indoor + room_coef * (walls[-1:] - indoor)
    live = lax.broadcasted_iota(jnp.int32, (1, slots), 1) < counts[0]
    wall_out[...] = jnp.where(live, jnp.concatenate([wall_first, middle, last], axis=0), walls)
    indoor_out[...] = jnp.where(live, indoor_new, indoor)
    heating = jnp.where(live, flux_coef * heat, 0.0)
    heating = jnp.concatenate([heating, jnp.zeros((deep - UL, slots), jnp.float32)], axis=0)
    spread = jnp.concatenate([jnp.where(cell_x == x, heating, 0.0) for x in range(x_size)], axis=0)
    added = dot(spread, at_y, ((1,), (1,)))
    for x in range(x_size):
        for t in range(deep // 8):
            out[pl.ds(8 * x_size * t + x, 8, stride=x_size), :] = (
                lower[x][8 * t : 8 * t + 8] + added[deep * x + 8 * t : deep * x + 8 * t + 8]
            )


def exchange(axis, to_a, to_b):
    size = lax.axis_size(axis)
    pairs_a = [(i, i + 1) for i in range(0, size, 2)]
    pairs_b = [(i, (i + 1) % size) for i in range(1, size, 2)]
    both = [pairs + [(j, i) for i, j in pairs] for pairs in (pairs_a, pairs_b)]
    return lax.ppermute(to_a, axis, both[0]), lax.ppermute(to_b, axis, both[1])


def per_device(
    scalars,
    winds,
    map_factor,
    urban_counts,
    urban_cols,
    street_class,
    area_table,
    wall_temp,
    indoor_temp,
):
    n_scalars, levels, x_size, y_size = scalars.shape
    slots = urban_cols.shape[0]
    rows = n_scalars * levels // CHUNKS
    f32 = functools.partial(jax.ShapeDtypeStruct, dtype=jnp.float32)
    field = scalars.reshape(n_scalars * levels * x_size, y_size)
    wind = winds.reshape(2 * levels * x_size, y_size)
    params = pltpu.CompilerParams(vmem_limit_bytes=40 * 2**20)
    whole = pl.BlockSpec(memory_space=pltpu.VMEM)

    smem = pl.BlockSpec(memory_space=pltpu.SMEM)
    hbm = pl.BlockSpec(memory_space=pltpu.HBM)
    odd = jnp.stack([lax.axis_index("gx") % 2, lax.axis_index("gy") % 2]).astype(jnp.int32)
    cheap = pl.CostEstimate(flops=1000, bytes_accessed=1000, transcendentals=0)

    pieces = 4
    first_rows = pl.pallas_call(
        functools.partial(first_rows_kernel, x_size, rows, levels, pieces),
        in_specs=[smem, hbm, hbm],
        out_specs=[whole] * 2,
        out_shape=[f32((WIDTH * rows + levels, y_size))] * 2,
        scratch_shapes=[
            pltpu.VMEM((rows * x_size, y_size), jnp.float32),
            pltpu.VMEM((levels * x_size, y_size), jnp.float32),
            pltpu.SemaphoreType.DMA((pieces + 1,)),
        ],
        compiler_params=params,
        cost_estimate=cheap,
        name="first_rows",
    )(odd, field, wind)
    received = [None] * CHUNKS
    received[0] = exchange("gx", *first_rows)
    for c in range(CHUNKS):
        extra = levels if c == 0 else 0
        outs = pl.pallas_call(
            functools.partial(extract_kernel, x_size, c, c == 0),
            in_specs=[smem, whole] + [whole] * (c == 0),
            out_specs=[whole] * (1 if c == 0 else 3),
            out_shape=[f32((WIDTH * rows, y_size))] * (0 if c == 0 else 2) + [f32((rows + extra, y_size))],
            compiler_params=params,
            cost_estimate=cheap,
            name=f"extract_{c}",
        )(odd, field, *([wind] if c == 0 else []))
        if c > 0:
            received[c] = exchange("gx", *outs[:2])
        received[c] = (*received[c], *exchange("gy", outs[-1], outs[-1]))

    speeds = pl.pallas_call(
        functools.partial(wind_kernel, x_size, rows),
        in_specs=[smem] + [whole] * 6,
        out_specs=[whole] * 6,
        out_shape=[
            f32((x_size + 1, levels, y_size)),
            f32((x_size, levels, y_size)),
            f32((x_size, levels, y_size)),
            f32((levels, y_size)),
            f32((levels, y_size)),
            f32((len(DIVISORS), x_size, 8, y_size)),
        ],
        compiler_params=params,
        cost_estimate=cheap,
        name="speeds",
    )(odd, wind, map_factor, *received[0])
    matrices = stencil_matrices(y_size)

    steps = rows // levels
    sections = [None] * CHUNKS
    result = None
    for k in range(len(DIVISORS)):
        last = k == len(DIVISORS) - 1
        for c in range(CHUNKS):
            operands = [odd] + ([field] if k == 0 else [sections[c], field])
            operands += [*received[c], *speeds, *matrices]
            specs = [smem] + [whole] * (len(operands) - 1)
            city = last and c == 0
            aliases = {}
            flat_c = pl.BlockSpec((levels * x_size, y_size), lambda g, c=c: (c * steps + g, 0))
            if city:
                operands += [
                    urban_counts,
                    urban_cols[None],
                    street_class[None],
                    area_table,
                    wall_temp,
                    indoor_temp[None],
                ]
                specs += [smem] + [whole] * 5
                out_specs = [flat_c, whole, whole]
                out_shape = [f32(field.shape), f32(wall_temp.shape), f32((1, slots))]
            elif last:
                aliases = {len(operands): 0}
                operands += [result]
                specs += [pl.BlockSpec(memory_space=pl.ANY)]
                out_specs = [flat_c]
                out_shape = [f32(field.shape)]
            else:
                out_specs = [whole] * 4
                out_shape = [
                    f32((x_size, rows, y_size)),
                    f32((WIDTH * rows, y_size)),
                    f32((WIDTH * rows, y_size)),
                    f32((rows, y_size)),
                ]
            outs = pl.pallas_call(
                functools.partial(section_kernel, x_size, k, c, last, city),
                grid=(steps,) if last else (),
                in_specs=specs,
                out_specs=out_specs,
                out_shape=out_shape,
                scratch_shapes=[pltpu.VMEM((levels, y_size), jnp.float32)]
                + [pltpu.VMEM((levels * x_size, y_size), jnp.float32)] * 4,
                input_output_aliases=aliases,
                compiler_params=params,
                cost_estimate=cheap,
                name=f"section_{k}_{c}",
            )(*operands)
            if city:
                result, wall_out, indoor_out = outs
            elif last:
                (result,) = outs
            else:
                sections[c], *outgoing, packed = outs
                received[c] = (*exchange("gx", *outgoing), *exchange("gy", packed, packed))
    return (result.reshape(scalars.shape), wall_out, indoor_out[0])


def solution(mesh):
    in_specs = (
        P(None, None, "gx", "gy"),
        P(None, None, "gx", "gy"),
        P("gx", "gy"),
        P(("gx", "gy")),
        P(("gx", "gy")),
        P(("gx", "gy")),
        P(),
        P(None, ("gx", "gy")),
        P(("gx", "gy")),
    )
    out_specs = (P(None, None, "gx", "gy"), P(None, ("gx", "gy")), P(("gx", "gy")))
    return jax.shard_map(
        per_device, mesh=mesh, in_specs=in_specs, out_specs=out_specs, check_vma=False
    )
```

```python
import functools

import jax
import jax.numpy as jnp
import ml_dtypes
import numpy as np
from jax import lax
from jax.experimental import pallas as pl
from jax.experimental.pallas import tpu as pltpu
from jax.sharding import PartitionSpec as P

UL = 10
NWL = 10
NCLS = 10
WIDTH = 3
GROUP = 8
CHUNKS = 2
PIECE = 512
UNROLL = 2
DIVISORS = (3.0, 2.0, 1.0)
HIGH = (1, -8, 37, 37, -8, 1)
DAMP = (-1, 5, -10, 10, -5, 1)

heat_coef = 0.5
wall_coef = 0.05
conduct = 0.3
inner_coef = 0.2
room_coef = 0.1
flux_coef = 0.5
face_scale = 0.5 / 60.0


def lane_index(shape):
    return lax.broadcasted_iota(jnp.int32, shape, 1)


def rolled(array, shift):
    return pltpu.roll(array, shift % array.shape[1], 1)


def pack_edges(packed, row, x):
    moved = rolled(row, GROUP * x + WIDTH)
    lane = lane_index(row.shape)
    here = (lane >= GROUP * x) & (lane < GROUP * x + 2 * WIDTH)
    return moved if packed is None else jnp.where(here, moved, packed)


def ahead(row, halo, lane, k):
    if k > 0:
        return rolled(jnp.where(lane < k, halo, row), -k)
    return rolled(jnp.where(lane >= row.shape[1] + k, halo, row), -k)


def first_rows_kernel(x_size, rows, levels, pieces, odd, field, wind, to_a, to_b, field_here, wind_here, sems):
    size = rows * x_size // pieces
    copies = [
        pltpu.make_async_copy(field.at[pl.ds(p * size, size), :], field_here.at[pl.ds(p * size, size), :], sems.at[p])
        for p in range(pieces)
    ]
    copies.append(pltpu.make_async_copy(wind.at[pl.ds(0, levels * x_size), :], wind_here, sems.at[pieces]))
    for copy in copies:
        copy.start()
    even = odd[0] == 0
    for p in range(pieces):
        copies[p].wait()
        for t in range(p * rows // pieces // 8, (p + 1) * rows // pieces // 8):
            for j in range(WIDTH):
                low = field_here[pl.ds(t * 8 * x_size + j, 8, stride=x_size), :]
                high = field_here[pl.ds(t * 8 * x_size + x_size - WIDTH + j, 8, stride=x_size), :]
                to_a[j * rows + t * 8 : j * rows + t * 8 + 8, :] = jnp.where(even, high, low)
                to_b[j * rows + t * 8 : j * rows + t * 8 + 8, :] = jnp.where(even, low, high)
    copies[pieces].wait()
    for t in range(levels // 8):
        low = wind_here[pl.ds(t * 8 * x_size, 8, stride=x_size), :]
        high = wind_here[pl.ds(t * 8 * x_size + x_size - 1, 8, stride=x_size), :]
        at = WIDTH * rows + t * 8
        to_a[at : at + 8, :] = jnp.where(even, high, low)
        to_b[at : at + 8, :] = jnp.where(even, low, high)


def extract_kernel(x_size, chunk, with_wind, odd, field, *refs):
    if with_wind:
        wind, packed = refs
    else:
        to_a, to_b, packed = refs
    rows = packed.shape[0]
    if with_wind:
        levels = wind.shape[0] // (2 * x_size)
        rows = rows - levels
    even = odd[0] == 0

    def one(t, carry):
        base = pl.multiple_of((chunk * rows + t * 8) * x_size, 8 * x_size)
        edges = None
        for x in range(x_size):
            edges = pack_edges(edges, field[pl.ds(base + x, 8, stride=x_size), :], x)
        packed[pl.ds(pl.multiple_of(t * 8, 8), 8), :] = edges
        if not with_wind:
            for j in range(WIDTH):
                low = field[pl.ds(base + j, 8, stride=x_size), :]
                high = field[pl.ds(base + x_size - WIDTH + j, 8, stride=x_size), :]
                at = pl.ds(pl.multiple_of(j * rows + t * 8, 8), 8)
                to_a[at, :] = jnp.where(even, high, low)
                to_b[at, :] = jnp.where(even, low, high)
        return carry

    lax.fori_loop(0, rows // 8, one, 0, unroll=4)
    if with_wind:

        def one_wind(t, carry):
            base = pl.multiple_of((levels + t * 8) * x_size, 8 * x_size)
            edges = None
            for x in range(x_size):
                edges = pack_edges(edges, wind[pl.ds(base + x, 8, stride=x_size), :], x)
            packed[pl.ds(pl.multiple_of(rows + t * 8, 8), 8), :] = edges
            return carry

        lax.fori_loop(0, levels // 8, one_wind, 0, unroll=4)


def join_packs(even, from_a, from_b):
    south = jnp.where(even, from_b, from_a)
    north = jnp.where(even, from_a, from_b)
    return jnp.where((lane_index(south.shape) & (GROUP - 1)) < WIDTH, south, north)


def wind_kernel(x_size, rows, odd, wind, factor, from_a, from_b, pack_a, pack_b, *outs):
    speed_x, ahead_y, behind_y, edge_ahead, edge_behind, scales = outs
    levels = speed_x.shape[1]
    even_x, even_y = odd[0] == 0, odd[1] == 0
    for x in range(x_size):
        mapped = factor[pl.ds(x, 1), :]
        for k, divisor in enumerate(DIVISORS):
            scales[k, x] = jnp.broadcast_to(mapped * mapped * (-1.0 / divisor), scales.shape[2:])

    def one(t, carry):
        base = pl.multiple_of(t * 8 * x_size, 8 * x_size)
        at = pl.ds(pl.multiple_of(t * 8, 8), 8)
        there = pl.ds(pl.multiple_of(WIDTH * rows + t * 8, 8), 8)
        before = jnp.where(even_x, from_b[there, :], from_a[there, :])
        east = jnp.where(even_x, from_a[there, :], from_b[there, :])
        for x in range(x_size + 1):
            now = east if x == x_size else wind[pl.ds(base + x, 8, stride=x_size), :]
            speed_x[x, at, :] = face_scale * (before + now)
            before = now
        base = base + levels * x_size
        lane = lane_index(before.shape)
        there = pl.ds(pl.multiple_of(rows + t * 8, 8), 8)
        halo = join_packs(even_y, pack_a[there, :], pack_b[there, :])
        forward, backward = None, None
        for x in range(x_size):
            row = wind[pl.ds(base + x, 8, stride=x_size), :]
            edge = rolled(halo, -(GROUP * x + WIDTH))
            front = face_scale * (row + ahead(row, edge, lane, 1))
            back = face_scale * (row + ahead(row, edge, lane, -1))
            ahead_y[x, at, :] = front
            behind_y[x, at, :] = back
            forward = pack_edges(forward, front, x)
            backward = pack_edges(backward, back, x)
        edge_ahead[at, :] = forward
        edge_behind[at, :] = backward
        return carry

    lax.fori_loop(0, levels // 8, one, 0, unroll=UNROLL)


def stencil_matrices(y_size):
    inner = np.zeros((y_size, 4 * y_size), np.float32)
    edges = np.zeros((y_size, 4 * y_size), np.float32)
    for part, (taps, offset) in enumerate(((HIGH, -2), (DAMP, -2), (HIGH, -3), (DAMP, -3))):
        for n, tap in enumerate(taps):
            k = n + offset
            for j in range(y_size):
                if 0 <= j + k < y_size:
                    inner[j + k, part * y_size + j] = tap
            for g in range(0, y_size, GROUP):
                for j in range(WIDTH):
                    if j + k < 0:
                        edges[g + WIDTH + j + k, part * y_size + g + WIDTH + j] = tap
                    if j - WIDTH + k >= 0:
                        edges[g + j + k, part * y_size + g + j] = tap
    return [jnp.asarray(np.concatenate([m, m]).astype(ml_dtypes.bfloat16)) for m in (inner, edges)]


def split_halves(values):
    leading = values.astype(jnp.bfloat16)
    trailing = (values - leading.astype(jnp.float32)).astype(jnp.bfloat16)
    return jnp.concatenate([leading, trailing], axis=1)


def stencil_product(halves, matrix, columns=slice(None)):
    return jnp.dot(halves, matrix[:, columns], preferred_element_type=jnp.float32)


def section_kernel(x_size, k, chunk, last, with_city, odd, *refs):
    refs = list(refs)
    first = k == 0
    section = refs.pop(0)
    base_ref = section if first else refs.pop(0)
    from_a, from_b, pack_a, pack_b = [refs.pop(0) for _ in range(4)]
    speed_x, ahead_y, behind_y, edge_ahead, edge_behind, scales = [refs.pop(0) for _ in range(6)]
    inner_matrix, edge_matrix = [refs.pop(0) for _ in range(2)]
    parts = refs[-4:]
    share = refs[-5]
    refs = refs[:-5]
    if last:
        if with_city:
            city = [refs.pop(0) for _ in range(6)]
            out, wall_out, indoor_out = refs
        else:
            refs.pop(0)
            (out,) = refs
    else:
        out, to_a, to_b, packed = refs
    levels, y_size = edge_ahead.shape
    chunk_rows = base_ref.shape[0] // (CHUNKS * x_size)
    even_x, even_y = odd[0] == 0, odd[1] == 0

    def block(g, carry):
        corner = pl.multiple_of((chunk * chunk_rows + g * levels) * x_size, levels * x_size)
        here = pl.multiple_of(g * levels, levels)
        for p in range(levels * x_size // PIECE):
            if first:
                values = section[pl.ds(pl.multiple_of(corner + p * PIECE, PIECE), PIECE), :]
            else:
                n = PIECE // levels
                values = section[p * n : (p + 1) * n, pl.ds(here, levels), :].reshape(PIECE, y_size)
            halves = split_halves(values)
            for pair in range(2):
                product = stencil_product(halves, inner_matrix, slice(2 * pair * y_size, 2 * (pair + 1) * y_size))
                for j, part in enumerate(parts[2 * pair : 2 * pair + 2]):
                    part[p * PIECE : (p + 1) * PIECE, :] = product[:, j * y_size : (j + 1) * y_size]
        halo = join_packs(even_y, pack_a[pl.ds(here, levels), :], pack_b[pl.ds(here, levels), :])
        product = stencil_product(split_halves(halo), edge_matrix)
        after, before = edge_ahead[...], edge_behind[...]
        share[...] = (
            after * product[:, :y_size]
            - jnp.abs(after) * product[:, y_size : 2 * y_size]
            - before * product[:, 2 * y_size : 3 * y_size]
            + jnp.abs(before) * product[:, 3 * y_size :]
        )

        def one(t, carry):
            at = pl.ds(pl.multiple_of(t * 8, 8), 8)
            rows_at = pl.ds(pl.multiple_of(here + t * 8, 8), 8)
            start = pl.multiple_of(corner + t * 8 * x_size, 8 * x_size)

            def halo_rows(mine, other, j):
                edge_at = pl.ds(pl.multiple_of(j * chunk_rows + here + t * 8, 8), 8)
                return jnp.where(even_x, mine[edge_at, :], other[edge_at, :])

            def cell(x):
                if x < 0:
                    return halo_rows(from_b, from_a, x + WIDTH)
                if x >= x_size:
                    return halo_rows(from_a, from_b, x - x_size)
                return section[pl.ds(start + x, 8, stride=x_size), :] if first else section[x, rows_at, :]

            lane = lane_index((8, y_size))
            edge_lane = (lane < WIDTH) | (lane >= y_size - WIDTH)
            edge_share = share[at, :]
            q = [cell(x) for x in range(-3, 2)]
            d1 = [q[i + 1] - q[i] for i in range(4)]
            d2 = [d1[i + 1] - d1[i] for i in range(3)]
            d3 = [d2[i + 1] - d2[i] for i in range(2)]
            d4 = d3[1] - d3[0]
            smooth = d4 - 5.0 * d2[1] + 30.0 * q[2]
            q, d1, d2, d3 = q[3:], d1[-1], d2[-1], d3[-1]
            flux_before = None
            edges, lows = None, []
            for x in range(-1, x_size):
                q.append(cell(x + WIDTH))
                new1 = q[-1] - q[-2]
                new2 = new1 - d1
                new3 = new2 - d2
                new4 = new3 - d3
                new_smooth = new4 - 5.0 * d2 + 30.0 * q[0]
                speed = speed_x[x + 1, at, :]
                flux = speed * (smooth + new_smooth) - jnp.abs(speed) * (new4 - d4)
                d1, d2, d3, d4, smooth = new1, new2, new3, new4, new_smooth
                if x >= 0:
                    if first:
                        lines = [part[pl.ds(t * 8 * x_size + x, 8, stride=x_size), :] for part in parts]
                    else:
                        lines = [part[pl.ds(pl.multiple_of(x * levels + t * 8, 8), 8), :] for part in parts]
                    after, before = ahead_y[x, at, :], behind_y[x, at, :]
                    moved = rolled(edge_share, -(GROUP * x + WIDTH))
                    divergence = (
                        (flux - flux_before)
                        + (after * lines[0] - jnp.abs(after) * lines[1])
                        - (before * lines[2] - jnp.abs(before) * lines[3])
                        + jnp.where(edge_lane, moved, 0.0)
                    )
                    base = base_ref[pl.ds(start + x, 8, stride=x_size), :]
                    new = base + scales[k, x] * divergence
                    if last:
                        out[pl.ds(pl.multiple_of(t * 8 * x_size, 8 * x_size) + x, 8, stride=x_size), :] = new
                    else:
                        out[x, rows_at, :] = new
                        edges = pack_edges(edges, new, x)
                        if x < WIDTH:
                            lows.append(new)
                        if x >= x_size - WIDTH:
                            j = x - x_size + WIDTH
                            edge_at = pl.ds(pl.multiple_of(j * chunk_rows + here + t * 8, 8), 8)
                            to_a[edge_at, :] = jnp.where(even_x, new, lows[j])
                            to_b[edge_at, :] = jnp.where(even_x, lows[j], new)
                flux_before = flux
                q = q[1:]
            if not last:
                packed[rows_at, :] = edges
            return carry

        lax.fori_loop(0, levels // 8, one, 0, unroll=UNROLL)
        return carry

    if last:
        block(pl.program_id(0), 0)
    else:
        lax.fori_loop(0, chunk_rows // levels, block, 0)
    if last and with_city:

        @pl.when(pl.program_id(0) == 0)
        def _():
            city_step(x_size, out, *city, wall_out, indoor_out)


def dot(a, b, dims):
    return lax.dot_general(
        a, b, (dims, ((), ())), precision=lax.Precision.HIGHEST, preferred_element_type=jnp.float32
    )


def city_step(x_size, out, counts, cols_ref, class_ref, table, wall_ref, indoor_ref, wall_out, indoor_out):
    deep = 16
    cols = cols_ref[...]
    slots = cols.shape[1]
    y_size = out.shape[1]
    cell_x = lax.div(cols, y_size)
    cell_y = lax.rem(cols, y_size)
    lower = [
        jnp.concatenate([out[pl.ds(8 * x_size * t + x, 8, stride=x_size), :] for t in range(deep // 8)], axis=0)
        for x in range(x_size)
    ]
    at_y = (lax.broadcasted_iota(jnp.int32, (y_size, slots), 0) == cell_y).astype(jnp.float32)
    gathered = dot(jnp.concatenate(lower, axis=0), at_y, ((1,), (0,)))
    air = jnp.zeros((deep, slots), jnp.float32)
    for x in range(x_size):
        air = jnp.where(cell_x == x, gathered[deep * x : deep * (x + 1)], air)
    air = air[:UL]
    onehot = (lax.broadcasted_iota(jnp.int32, (NCLS, slots), 0) == class_ref[...]).astype(jnp.float32)
    areas = dot(table[...], onehot, ((0,), (0,)))
    walls = wall_ref[...]
    indoor = indoor_ref[...]
    heat = heat_coef * areas * (walls[0:1] - air)
    wall_first = walls[0:1] - wall_coef * jnp.sum(heat, axis=0, keepdims=True) + conduct * (walls[1:2] - walls[0:1])
    middle = walls[1:-1] + conduct * (walls[:-2] - 2.0 * walls[1:-1] + walls[2:])
    last = walls[-1:] + conduct * (walls[-2:-1] - walls[-1:]) + inner_coef * (indoor - walls[-1:])
    indoor_new = indoor + room_coef * (walls[-1:] - indoor)
    live = lax.broadcasted_iota(jnp.int32, (1, slots), 1) < counts[0]
    wall_out[...] = jnp.where(live, jnp.concatenate([wall_first, middle, last], axis=0), walls)
    indoor_out[...] = jnp.where(live, indoor_new, indoor)
    heating = jnp.where(live, flux_coef * heat, 0.0)
    heating = jnp.concatenate([heating, jnp.zeros((deep - UL, slots), jnp.float32)], axis=0)
    spread = jnp.concatenate([jnp.where(cell_x == x, heating, 0.0) for x in range(x_size)], axis=0)
    added = dot(spread, at_y, ((1,), (1,)))
    for x in range(x_size):
        for t in range(deep // 8):
            out[pl.ds(8 * x_size * t + x, 8, stride=x_size), :] = (
                lower[x][8 * t : 8 * t + 8] + added[deep * x + 8 * t : deep * x + 8 * t + 8]
            )


def exchange(axis, to_a, to_b):
    size = lax.axis_size(axis)
    pairs_a = [(i, i + 1) for i in range(0, size, 2)]
    pairs_b = [(i, (i + 1) % size) for i in range(1, size, 2)]
    both = [pairs + [(j, i) for i, j in pairs] for pairs in (pairs_a, pairs_b)]
    return lax.ppermute(to_a, axis, both[0]), lax.ppermute(to_b, axis, both[1])


def per_device(
    scalars,
    winds,
    map_factor,
    urban_counts,
    urban_cols,
    street_class,
    area_table,
    wall_temp,
    indoor_temp,
):
    n_scalars, levels, x_size, y_size = scalars.shape
    slots = urban_cols.shape[0]
    rows = n_scalars * levels // CHUNKS
    f32 = functools.partial(jax.ShapeDtypeStruct, dtype=jnp.float32)
    field = scalars.reshape(n_scalars * levels * x_size, y_size)
    wind = winds.reshape(2 * levels * x_size, y_size)
    params = pltpu.CompilerParams(vmem_limit_bytes=40 * 2**20)
    whole = pl.BlockSpec(memory_space=pltpu.VMEM)

    smem = pl.BlockSpec(memory_space=pltpu.SMEM)
    hbm = pl.BlockSpec(memory_space=pltpu.HBM)
    odd = jnp.stack([lax.axis_index("gx") % 2, lax.axis_index("gy") % 2]).astype(jnp.int32)
    cheap = pl.CostEstimate(flops=1000, bytes_accessed=1000, transcendentals=0)

    pieces = 4
    first_rows = pl.pallas_call(
        functools.partial(first_rows_kernel, x_size, rows, levels, pieces),
        in_specs=[smem, hbm, hbm],
        out_specs=[whole] * 2,
        out_shape=[f32((WIDTH * rows + levels, y_size))] * 2,
        scratch_shapes=[
            pltpu.VMEM((rows * x_size, y_size), jnp.float32),
            pltpu.VMEM((levels * x_size, y_size), jnp.float32),
            pltpu.SemaphoreType.DMA((pieces + 1,)),
        ],
        compiler_params=pltpu.CompilerParams(vmem_limit_bytes=62 * 2**20),
        cost_estimate=cheap,
        name="first_rows",
    )(odd, field, wind)
    received = [None] * CHUNKS
    received[0] = exchange("gx", *first_rows)
    for c in range(CHUNKS):
        extra = levels if c == 0 else 0
        outs = pl.pallas_call(
            functools.partial(extract_kernel, x_size, c, c == 0),
            in_specs=[smem, whole] + [whole] * (c == 0),
            out_specs=[whole] * (1 if c == 0 else 3),
            out_shape=[f32((WIDTH * rows, y_size))] * (0 if c == 0 else 2) + [f32((rows + extra, y_size))],
            compiler_params=params,
            cost_estimate=cheap,
            name=f"extract_{c}",
        )(odd, field, *([wind] if c == 0 else []))
        if c > 0:
            received[c] = exchange("gx", *outs[:2])
        received[c] = (*received[c], *exchange("gy", outs[-1], outs[-1]))

    speeds = pl.pallas_call(
        functools.partial(wind_kernel, x_size, rows),
        in_specs=[smem] + [whole] * 6,
        out_specs=[whole] * 6,
        out_shape=[
            f32((x_size + 1, levels, y_size)),
            f32((x_size, levels, y_size)),
            f32((x_size, levels, y_size)),
            f32((levels, y_size)),
            f32((levels, y_size)),
            f32((len(DIVISORS), x_size, 8, y_size)),
        ],
        compiler_params=params,
        cost_estimate=cheap,
        name="speeds",
    )(odd, wind, map_factor, *received[0])
    matrices = stencil_matrices(y_size)

    steps = rows // levels
    sections = [None] * CHUNKS
    result = None
    for k in range(len(DIVISORS)):
        last = k == len(DIVISORS) - 1
        for c in range(CHUNKS):
            operands = [odd] + ([field] if k == 0 else [sections[c], field])
            operands += [*received[c], *speeds, *matrices]
            specs = [smem] + [whole] * (len(operands) - 1)
            city = last and c == 0
            aliases = {}
            flat_c = pl.BlockSpec((levels * x_size, y_size), lambda g, c=c: (c * steps + g, 0))
            if city:
                operands += [
                    urban_counts,
                    urban_cols[None],
                    street_class[None],
                    area_table,
                    wall_temp,
                    indoor_temp[None],
                ]
                specs += [smem] + [whole] * 5
                out_specs = [flat_c, whole, whole]
                out_shape = [f32(field.shape), f32(wall_temp.shape), f32((1, slots))]
            elif last:
                aliases = {len(operands): 0}
                operands += [result]
                specs += [pl.BlockSpec(memory_space=pl.ANY)]
                out_specs = [flat_c]
                out_shape = [f32(field.shape)]
            else:
                out_specs = [whole] * 4
                out_shape = [
                    f32((x_size, rows, y_size)),
                    f32((WIDTH * rows, y_size)),
                    f32((WIDTH * rows, y_size)),
                    f32((rows, y_size)),
                ]
            outs = pl.pallas_call(
                functools.partial(section_kernel, x_size, k, c, last, city),
                grid=(steps,) if last else (),
                in_specs=specs,
                out_specs=out_specs,
                out_shape=out_shape,
                scratch_shapes=[pltpu.VMEM((levels, y_size), jnp.float32)]
                + [pltpu.VMEM((levels * x_size, y_size), jnp.float32)] * 4,
                input_output_aliases=aliases,
                compiler_params=params,
                cost_estimate=cheap,
                name=f"section_{k}_{c}",
            )(*operands)
            if city:
                result, wall_out, indoor_out = outs
            elif last:
                (result,) = outs
            else:
                sections[c], *outgoing, packed = outs
                received[c] = (*exchange("gx", *outgoing), *exchange("gy", packed, packed))
    return (result.reshape(scalars.shape), wall_out, indoor_out[0])


def solution(mesh):
    in_specs = (
        P(None, None, "gx", "gy"),
        P(None, None, "gx", "gy"),
        P("gx", "gy"),
        P(("gx", "gy")),
        P(("gx", "gy")),
        P(("gx", "gy")),
        P(),
        P(None, ("gx", "gy")),
        P(("gx", "gy")),
    )
    out_specs = (P(None, None, "gx", "gy"), P(None, ("gx", "gy")), P(("gx", "gy")))
    return jax.shard_map(
        per_device, mesh=mesh, in_specs=in_specs, out_specs=out_specs, check_vma=False
    )
```

```python
import functools

import jax
import jax.numpy as jnp
import ml_dtypes
import numpy as np
from jax import lax
from jax.experimental import pallas as pl
from jax.experimental.pallas import tpu as pltpu
from jax.sharding import PartitionSpec as P

UL = 10
NWL = 10
NCLS = 10
WIDTH = 3
GROUP = 8
CHUNKS = 2
PIECE = 512
UNROLL = 2
DIVISORS = (3.0, 2.0, 1.0)
HIGH = (1, -8, 37, 37, -8, 1)
DAMP = (-1, 5, -10, 10, -5, 1)

heat_coef = 0.5
wall_coef = 0.05
conduct = 0.3
inner_coef = 0.2
room_coef = 0.1
flux_coef = 0.5
face_scale = 0.5 / 60.0


def lane_index(shape):
    return lax.broadcasted_iota(jnp.int32, shape, 1)


def rolled(array, shift):
    return pltpu.roll(array, shift % array.shape[1], 1)


def pack_edges(packed, row, x):
    moved = rolled(row, GROUP * x + WIDTH)
    lane = lane_index(row.shape)
    here = (lane >= GROUP * x) & (lane < GROUP * x + 2 * WIDTH)
    return moved if packed is None else jnp.where(here, moved, packed)


def ahead(row, halo, lane, k):
    if k > 0:
        return rolled(jnp.where(lane < k, halo, row), -k)
    return rolled(jnp.where(lane >= row.shape[1] + k, halo, row), -k)


def even_index(axis):
    return lax.rem(lax.axis_index(axis), 2) == 0


def first_rows_kernel(x_size, rows, levels, pieces, field, wind, to_a, to_b, field_here, wind_here, sems):
    size = rows * x_size // pieces
    copies = [
        pltpu.make_async_copy(field.at[pl.ds(p * size, size), :], field_here.at[pl.ds(p * size, size), :], sems.at[p])
        for p in range(pieces)
    ]
    copies.append(pltpu.make_async_copy(wind.at[pl.ds(0, levels * x_size), :], wind_here, sems.at[pieces]))
    for copy in copies:
        copy.start()
    even = even_index("gx")
    for p in range(pieces):
        copies[p].wait()
        for t in range(p * rows // pieces // 8, (p + 1) * rows // pieces // 8):
            for j in range(WIDTH):
                low = field_here[pl.ds(t * 8 * x_size + j, 8, stride=x_size), :]
                high = field_here[pl.ds(t * 8 * x_size + x_size - WIDTH + j, 8, stride=x_size), :]
                to_a[j * rows + t * 8 : j * rows + t * 8 + 8, :] = jnp.where(even, high, low)
                to_b[j * rows + t * 8 : j * rows + t * 8 + 8, :] = jnp.where(even, low, high)
    copies[pieces].wait()
    for t in range(levels // 8):
        low = wind_here[pl.ds(t * 8 * x_size, 8, stride=x_size), :]
        high = wind_here[pl.ds(t * 8 * x_size + x_size - 1, 8, stride=x_size), :]
        at = WIDTH * rows + t * 8
        to_a[at : at + 8, :] = jnp.where(even, high, low)
        to_b[at : at + 8, :] = jnp.where(even, low, high)


def extract_kernel(x_size, chunk, with_wind, field, *refs):
    if with_wind:
        wind, packed = refs
    else:
        to_a, to_b, packed = refs
    rows = packed.shape[0]
    if with_wind:
        levels = wind.shape[0] // (2 * x_size)
        rows = rows - levels
    even = even_index("gx")

    def one(t, carry):
        base = pl.multiple_of((chunk * rows + t * 8) * x_size, 8 * x_size)
        edges = None
        for x in range(x_size):
            edges = pack_edges(edges, field[pl.ds(base + x, 8, stride=x_size), :], x)
        packed[pl.ds(pl.multiple_of(t * 8, 8), 8), :] = edges
        if not with_wind:
            for j in range(WIDTH):
                low = field[pl.ds(base + j, 8, stride=x_size), :]
                high = field[pl.ds(base + x_size - WIDTH + j, 8, stride=x_size), :]
                at = pl.ds(pl.multiple_of(j * rows + t * 8, 8), 8)
                to_a[at, :] = jnp.where(even, high, low)
                to_b[at, :] = jnp.where(even, low, high)
        return carry

    lax.fori_loop(0, rows // 8, one, 0, unroll=4)
    if with_wind:

        def one_wind(t, carry):
            base = pl.multiple_of((levels + t * 8) * x_size, 8 * x_size)
            edges = None
            for x in range(x_size):
                edges = pack_edges(edges, wind[pl.ds(base + x, 8, stride=x_size), :], x)
            packed[pl.ds(pl.multiple_of(rows + t * 8, 8), 8), :] = edges
            return carry

        lax.fori_loop(0, levels // 8, one_wind, 0, unroll=4)


def join_packs(even, from_a, from_b):
    south = jnp.where(even, from_b, from_a)
    north = jnp.where(even, from_a, from_b)
    return jnp.where((lane_index(south.shape) & (GROUP - 1)) < WIDTH, south, north)


def wind_kernel(x_size, rows, wind, factor, pack_a, pack_b, *outs):
    speed_x, ahead_y, behind_y, edge_ahead, edge_behind, scales = outs
    levels = speed_x.shape[1]
    even_y = even_index("gy")
    for x in range(x_size):
        mapped = factor[pl.ds(x, 1), :]
        for k, divisor in enumerate(DIVISORS):
            scales[k, x] = jnp.broadcast_to(mapped * mapped * (-1.0 / divisor), scales.shape[2:])

    def one(t, carry):
        base = pl.multiple_of(t * 8 * x_size, 8 * x_size)
        at = pl.ds(pl.multiple_of(t * 8, 8), 8)
        before = jnp.zeros((8, wind.shape[1]), jnp.float32)
        for x in range(x_size + 1):
            now = jnp.zeros_like(before) if x == x_size else wind[pl.ds(base + x, 8, stride=x_size), :]
            speed_x[x, at, :] = face_scale * (before + now)
            before = now
        base = base + levels * x_size
        lane = lane_index(before.shape)
        there = pl.ds(pl.multiple_of(rows + t * 8, 8), 8)
        halo = join_packs(even_y, pack_a[there, :], pack_b[there, :])
        forward, backward = None, None
        for x in range(x_size):
            row = wind[pl.ds(base + x, 8, stride=x_size), :]
            edge = rolled(halo, -(GROUP * x + WIDTH))
            front = face_scale * (row + ahead(row, edge, lane, 1))
            back = face_scale * (row + ahead(row, edge, lane, -1))
            ahead_y[x, at, :] = front
            behind_y[x, at, :] = back
            forward = pack_edges(forward, front, x)
            backward = pack_edges(backward, back, x)
        edge_ahead[at, :] = forward
        edge_behind[at, :] = backward
        return carry

    lax.fori_loop(0, levels // 8, one, 0, unroll=UNROLL)


def stencil_matrices(y_size):
    inner = np.zeros((y_size, 4 * y_size), np.float32)
    edges = np.zeros((y_size, 4 * y_size), np.float32)
    for part, (taps, offset) in enumerate(((HIGH, -2), (DAMP, -2), (HIGH, -3), (DAMP, -3))):
        for n, tap in enumerate(taps):
            k = n + offset
            for j in range(y_size):
                if 0 <= j + k < y_size:
                    inner[j + k, part * y_size + j] = tap
            for g in range(0, y_size, GROUP):
                for j in range(WIDTH):
                    if j + k < 0:
                        edges[g + WIDTH + j + k, part * y_size + g + WIDTH + j] = tap
                    if j - WIDTH + k >= 0:
                        edges[g + j + k, part * y_size + g + j] = tap
    return [jnp.asarray(np.concatenate([m, m]).astype(ml_dtypes.bfloat16)) for m in (inner, edges)]


def split_halves(values):
    leading = values.astype(jnp.bfloat16)
    trailing = (values - leading.astype(jnp.float32)).astype(jnp.bfloat16)
    return jnp.concatenate([leading, trailing], axis=1)


def stencil_product(halves, matrix, columns=slice(None)):
    return jnp.dot(halves, matrix[:, columns], preferred_element_type=jnp.float32)


def section_kernel(x_size, k, chunk, last, with_city, *refs):
    refs = list(refs)
    first = k == 0
    section = refs.pop(0)
    base_ref = section if first else refs.pop(0)
    from_a, from_b, pack_a, pack_b = [refs.pop(0) for _ in range(4)]
    wind_a, wind_b = [refs.pop(0) for _ in range(2)]
    speed_x, ahead_y, behind_y, edge_ahead, edge_behind, scales = [refs.pop(0) for _ in range(6)]
    inner_matrix, edge_matrix = [refs.pop(0) for _ in range(2)]
    parts = refs[-4:]
    share = refs[-5]
    refs = refs[:-5]
    if last:
        if with_city:
            city = [refs.pop(0) for _ in range(6)]
            out, wall_out, indoor_out = refs
        else:
            refs.pop(0)
            (out,) = refs
    else:
        out, to_a, to_b, packed = refs
    levels, y_size = edge_ahead.shape
    chunk_rows = base_ref.shape[0] // (CHUNKS * x_size)
    even_x, even_y = even_index("gx"), even_index("gy")

    def block(g, carry):
        corner = pl.multiple_of((chunk * chunk_rows + g * levels) * x_size, levels * x_size)
        here = pl.multiple_of(g * levels, levels)
        for p in range(levels * x_size // PIECE):
            n = PIECE // levels
            if first:
                lines = [section[pl.ds(corner + x, levels, stride=x_size), :] for x in range(p * n, (p + 1) * n)]
                values = jnp.concatenate(lines, axis=0)
            else:
                values = section[p * n : (p + 1) * n, pl.ds(here, levels), :].reshape(PIECE, y_size)
            halves = split_halves(values)
            for pair in range(2):
                product = stencil_product(halves, inner_matrix, slice(2 * pair * y_size, 2 * (pair + 1) * y_size))
                for j, part in enumerate(parts[2 * pair : 2 * pair + 2]):
                    part[p * PIECE : (p + 1) * PIECE, :] = product[:, j * y_size : (j + 1) * y_size]
        halo = join_packs(even_y, pack_a[pl.ds(here, levels), :], pack_b[pl.ds(here, levels), :])
        product = stencil_product(split_halves(halo), edge_matrix)
        after, before = edge_ahead[...], edge_behind[...]
        share[...] = (
            after * product[:, :y_size]
            - jnp.abs(after) * product[:, y_size : 2 * y_size]
            - before * product[:, 2 * y_size : 3 * y_size]
            + jnp.abs(before) * product[:, 3 * y_size :]
        )

        def one(t, carry):
            at = pl.ds(pl.multiple_of(t * 8, 8), 8)
            rows_at = pl.ds(pl.multiple_of(here + t * 8, 8), 8)
            start = pl.multiple_of(corner + t * 8 * x_size, 8 * x_size)

            def halo_rows(mine, other, j):
                edge_at = pl.ds(pl.multiple_of(j * chunk_rows + here + t * 8, 8), 8)
                return jnp.where(even_x, mine[edge_at, :], other[edge_at, :])

            def outer_wind(mine, other):
                wind_at = pl.ds(pl.multiple_of(WIDTH * chunk_rows + t * 8, 8), 8)
                return jnp.where(even_x, mine[wind_at, :], other[wind_at, :])

            def cell(x):
                if x < 0:
                    return halo_rows(from_b, from_a, x + WIDTH)
                if x >= x_size:
                    return halo_rows(from_a, from_b, x - x_size)
                return section[pl.ds(start + x, 8, stride=x_size), :] if first else section[x, rows_at, :]

            lane = lane_index((8, y_size))
            edge_lane = (lane < WIDTH) | (lane >= y_size - WIDTH)
            edge_share = share[at, :]
            q = [cell(x) for x in range(-3, 2)]
            d1 = [q[i + 1] - q[i] for i in range(4)]
            d2 = [d1[i + 1] - d1[i] for i in range(3)]
            d3 = [d2[i + 1] - d2[i] for i in range(2)]
            d4 = d3[1] - d3[0]
            smooth = d4 - 5.0 * d2[1] + 30.0 * q[2]
            q, d1, d2, d3 = q[3:], d1[-1], d2[-1], d3[-1]
            flux_before = None
            edges, lows = None, []
            for x in range(-1, x_size):
                q.append(cell(x + WIDTH))
                new1 = q[-1] - q[-2]
                new2 = new1 - d1
                new3 = new2 - d2
                new4 = new3 - d3
                new_smooth = new4 - 5.0 * d2 + 30.0 * q[0]
                speed = speed_x[x + 1, at, :]
                if x == -1:
                    speed = speed + face_scale * outer_wind(wind_b, wind_a)
                if x == x_size - 1:
                    speed = speed + face_scale * outer_wind(wind_a, wind_b)
                flux = speed * (smooth + new_smooth) - jnp.abs(speed) * (new4 - d4)
                d1, d2, d3, d4, smooth = new1, new2, new3, new4, new_smooth
                if x >= 0:
                    lines = [part[pl.ds(pl.multiple_of(x * levels + t * 8, 8), 8), :] for part in parts]
                    after, before = ahead_y[x, at, :], behind_y[x, at, :]
                    moved = rolled(edge_share, -(GROUP * x + WIDTH))
                    divergence = (
                        (flux - flux_before)
                        + (after * lines[0] - jnp.abs(after) * lines[1])
                        - (before * lines[2] - jnp.abs(before) * lines[3])
                        + jnp.where(edge_lane, moved, 0.0)
                    )
                    base = base_ref[pl.ds(start + x, 8, stride=x_size), :]
                    new = base + scales[k, x] * divergence
                    if last:
                        out[pl.ds(pl.multiple_of(t * 8 * x_size, 8 * x_size) + x, 8, stride=x_size), :] = new
                    else:
                        out[x, rows_at, :] = new
                        edges = pack_edges(edges, new, x)
                        if x < WIDTH:
                            lows.append(new)
                        if x >= x_size - WIDTH:
                            j = x - x_size + WIDTH
                            edge_at = pl.ds(pl.multiple_of(j * chunk_rows + here + t * 8, 8), 8)
                            to_a[edge_at, :] = jnp.where(even_x, new, lows[j])
                            to_b[edge_at, :] = jnp.where(even_x, lows[j], new)
                flux_before = flux
                q = q[1:]
            if not last:
                packed[rows_at, :] = edges
            return carry

        lax.fori_loop(0, levels // 8, one, 0, unroll=UNROLL)
        return carry

    if last:
        block(pl.program_id(0), 0)
    else:
        lax.fori_loop(0, chunk_rows // levels, block, 0)
    if last and with_city:

        @pl.when(pl.program_id(0) == 0)
        def _():
            city_step(x_size, out, *city, wall_out, indoor_out)


def dot(a, b, dims):
    return lax.dot_general(
        a, b, (dims, ((), ())), precision=lax.Precision.HIGHEST, preferred_element_type=jnp.float32
    )


def city_step(x_size, out, counts, cols_ref, class_ref, table, wall_ref, indoor_ref, wall_out, indoor_out):
    deep = 16
    cols = cols_ref[...]
    slots = cols.shape[1]
    y_size = out.shape[1]
    cell_x = lax.div(cols, y_size)
    cell_y = lax.rem(cols, y_size)
    lower = [
        jnp.concatenate([out[pl.ds(8 * x_size * t + x, 8, stride=x_size), :] for t in range(deep // 8)], axis=0)
        for x in range(x_size)
    ]
    at_y = (lax.broadcasted_iota(jnp.int32, (y_size, slots), 0) == cell_y).astype(jnp.float32)
    gathered = dot(jnp.concatenate(lower, axis=0), at_y, ((1,), (0,)))
    air = jnp.zeros((deep, slots), jnp.float32)
    for x in range(x_size):
        air = jnp.where(cell_x == x, gathered[deep * x : deep * (x + 1)], air)
    air = air[:UL]
    onehot = (lax.broadcasted_iota(jnp.int32, (NCLS, slots), 0) == class_ref[...]).astype(jnp.float32)
    areas = dot(table[...], onehot, ((0,), (0,)))
    walls = wall_ref[...]
    indoor = indoor_ref[...]
    heat = heat_coef * areas * (walls[0:1] - air)
    wall_first = walls[0:1] - wall_coef * jnp.sum(heat, axis=0, keepdims=True) + conduct * (walls[1:2] - walls[0:1])
    middle = walls[1:-1] + conduct * (walls[:-2] - 2.0 * walls[1:-1] + walls[2:])
    last = walls[-1:] + conduct * (walls[-2:-1] - walls[-1:]) + inner_coef * (indoor - walls[-1:])
    indoor_new = indoor + room_coef * (walls[-1:] - indoor)
    live = lax.broadcasted_iota(jnp.int32, (1, slots), 1) < counts[0]
    wall_out[...] = jnp.where(live, jnp.concatenate([wall_first, middle, last], axis=0), walls)
    indoor_out[...] = jnp.where(live, indoor_new, indoor)
    heating = jnp.where(live, flux_coef * heat, 0.0)
    heating = jnp.concatenate([heating, jnp.zeros((deep - UL, slots), jnp.float32)], axis=0)
    spread = jnp.concatenate([jnp.where(cell_x == x, heating, 0.0) for x in range(x_size)], axis=0)
    added = dot(spread, at_y, ((1,), (1,)))
    for x in range(x_size):
        for t in range(deep // 8):
            out[pl.ds(8 * x_size * t + x, 8, stride=x_size), :] = (
                lower[x][8 * t : 8 * t + 8] + added[deep * x + 8 * t : deep * x + 8 * t + 8]
            )


def exchange(axis, to_a, to_b):
    size = lax.axis_size(axis)
    pairs_a = [(i, i + 1) for i in range(0, size, 2)]
    pairs_b = [(i, (i + 1) % size) for i in range(1, size, 2)]
    both = [pairs + [(j, i) for i, j in pairs] for pairs in (pairs_a, pairs_b)]
    return lax.ppermute(to_a, axis, both[0]), lax.ppermute(to_b, axis, both[1])


def per_device(
    scalars,
    winds,
    map_factor,
    urban_counts,
    urban_cols,
    street_class,
    area_table,
    wall_temp,
    indoor_temp,
):
    n_scalars, levels, x_size, y_size = scalars.shape
    slots = urban_cols.shape[0]
    rows = n_scalars * levels // CHUNKS
    f32 = functools.partial(jax.ShapeDtypeStruct, dtype=jnp.float32)
    field = scalars.reshape(n_scalars * levels * x_size, y_size)
    wind = winds.reshape(2 * levels * x_size, y_size)
    params = pltpu.CompilerParams(vmem_limit_bytes=40 * 2**20)
    whole = pl.BlockSpec(memory_space=pltpu.VMEM)

    smem = pl.BlockSpec(memory_space=pltpu.SMEM)
    hbm = pl.BlockSpec(memory_space=pltpu.HBM)
    cheap = pl.CostEstimate(flops=1000, bytes_accessed=1000, transcendentals=0)

    pieces = 4
    first_rows = pl.pallas_call(
        functools.partial(first_rows_kernel, x_size, rows, levels, pieces),
        in_specs=[hbm, hbm],
        out_specs=[whole] * 2,
        out_shape=[f32((WIDTH * rows + levels, y_size))] * 2,
        scratch_shapes=[
            pltpu.VMEM((rows * x_size, y_size), jnp.float32),
            pltpu.VMEM((levels * x_size, y_size), jnp.float32),
            pltpu.SemaphoreType.DMA((pieces + 1,)),
        ],
        compiler_params=pltpu.CompilerParams(vmem_limit_bytes=62 * 2**20),
        cost_estimate=cheap,
        name="first_rows",
    )(field, wind)
    received = [None] * CHUNKS
    received[0] = exchange("gx", *first_rows)
    for c in range(CHUNKS):
        extra = levels if c == 0 else 0
        outs = pl.pallas_call(
            functools.partial(extract_kernel, x_size, c, c == 0),
            in_specs=[whole] + [whole] * (c == 0),
            out_specs=[whole] * (1 if c == 0 else 3),
            out_shape=[f32((WIDTH * rows, y_size))] * (0 if c == 0 else 2) + [f32((rows + extra, y_size))],
            compiler_params=params,
            cost_estimate=cheap,
            name=f"extract_{c}",
        )(field, *([wind] if c == 0 else []))
        if c > 0:
            received[c] = exchange("gx", *outs[:2])
        received[c] = (*received[c], *exchange("gy", outs[-1], outs[-1]))

    speeds = pl.pallas_call(
        functools.partial(wind_kernel, x_size, rows),
        in_specs=[whole] * 4,
        out_specs=[whole] * 6,
        out_shape=[
            f32((x_size + 1, levels, y_size)),
            f32((x_size, levels, y_size)),
            f32((x_size, levels, y_size)),
            f32((levels, y_size)),
            f32((levels, y_size)),
            f32((len(DIVISORS), x_size, 8, y_size)),
        ],
        compiler_params=params,
        cost_estimate=cheap,
        name="speeds",
    )(wind, map_factor, *received[0][2:])
    winds_beyond = received[0][:2]
    matrices = stencil_matrices(y_size)

    steps = rows // levels
    sections = [None] * CHUNKS
    result = None
    for k in range(len(DIVISORS)):
        last = k == len(DIVISORS) - 1
        for c in range(CHUNKS):
            operands = [field] if k == 0 else [sections[c], field]
            operands += [*received[c], *winds_beyond, *speeds, *matrices]
            specs = [whole] * len(operands)
            city = last and c == 0
            aliases = {}
            flat_c = pl.BlockSpec((levels * x_size, y_size), lambda g, c=c: (c * steps + g, 0))
            if city:
                operands += [
                    urban_counts,
                    urban_cols[None],
                    street_class[None],
                    area_table,
                    wall_temp,
                    indoor_temp[None],
                ]
                specs += [smem] + [whole] * 5
                out_specs = [flat_c, whole, whole]
                out_shape = [f32(field.shape), f32(wall_temp.shape), f32((1, slots))]
            elif last:
                aliases = {len(operands): 0}
                operands += [result]
                specs += [pl.BlockSpec(memory_space=pl.ANY)]
                out_specs = [flat_c]
                out_shape = [f32(field.shape)]
            else:
                out_specs = [whole] * 4
                out_shape = [
                    f32((x_size, rows, y_size)),
                    f32((WIDTH * rows, y_size)),
                    f32((WIDTH * rows, y_size)),
                    f32((rows, y_size)),
                ]
            outs = pl.pallas_call(
                functools.partial(section_kernel, x_size, k, c, last, city),
                grid=(steps,) if last else (),
                in_specs=specs,
                out_specs=out_specs,
                out_shape=out_shape,
                scratch_shapes=[pltpu.VMEM((levels, y_size), jnp.float32)]
                + [pltpu.VMEM((levels * x_size, y_size), jnp.float32)] * 4,
                input_output_aliases=aliases,
                compiler_params=params,
                cost_estimate=cheap,
                name=f"section_{k}_{c}",
            )(*operands)
            if city:
                result, wall_out, indoor_out = outs
            elif last:
                (result,) = outs
            else:
                sections[c], *outgoing, packed = outs
                received[c] = (*exchange("gx", *outgoing), *exchange("gy", packed, packed))
    return (result.reshape(scalars.shape), wall_out, indoor_out[0])


def solution(mesh):
    in_specs = (
        P(None, None, "gx", "gy"),
        P(None, None, "gx", "gy"),
        P("gx", "gy"),
        P(("gx", "gy")),
        P(("gx", "gy")),
        P(("gx", "gy")),
        P(),
        P(None, ("gx", "gy")),
        P(("gx", "gy")),
    )
    out_specs = (P(None, None, "gx", "gy"), P(None, ("gx", "gy")), P(("gx", "gy")))
    return jax.shard_map(
        per_device, mesh=mesh, in_specs=in_specs, out_specs=out_specs, check_vma=False
    )
```

```python
import functools

import jax
import jax.numpy as jnp
import ml_dtypes
import numpy as np
from jax import lax
from jax.experimental import pallas as pl
from jax.experimental.pallas import tpu as pltpu
from jax.sharding import PartitionSpec as P

UL = 10
NWL = 10
NCLS = 10
WIDTH = 3
GROUP = 8
CHUNKS = 2
PIECE = 512
UNROLL = 2
DIVISORS = (3.0, 2.0, 1.0)
HIGH = (1, -8, 37, 37, -8, 1)
DAMP = (-1, 5, -10, 10, -5, 1)

heat_coef = 0.5
wall_coef = 0.05
conduct = 0.3
inner_coef = 0.2
room_coef = 0.1
flux_coef = 0.5
face_scale = 0.5 / 60.0


def lane_index(shape):
    return lax.broadcasted_iota(jnp.int32, shape, 1)


def rolled(array, shift):
    return pltpu.roll(array, shift % array.shape[1], 1)


def pack_edges(packed, row, x):
    moved = rolled(row, GROUP * x + WIDTH)
    lane = lane_index(row.shape)
    here = (lane >= GROUP * x) & (lane < GROUP * x + 2 * WIDTH)
    return moved if packed is None else jnp.where(here, moved, packed)


def ahead(row, halo, lane, k):
    if k > 0:
        return rolled(jnp.where(lane < k, halo, row), -k)
    return rolled(jnp.where(lane >= row.shape[1] + k, halo, row), -k)


AFTER_FIRST = {"gx": 1, "gy": 0}


def after_in_a(axis):
    return lax.rem(lax.axis_index(axis), 2) == AFTER_FIRST[axis]


def first_rows_kernel(x_size, rows, levels, pieces, field, wind, to_a, to_b, field_here, wind_here, sems):
    size = rows * x_size // pieces
    copies = [
        pltpu.make_async_copy(field.at[pl.ds(p * size, size), :], field_here.at[pl.ds(p * size, size), :], sems.at[p])
        for p in range(pieces)
    ]
    copies.append(pltpu.make_async_copy(wind.at[pl.ds(0, levels * x_size), :], wind_here, sems.at[pieces]))
    for copy in copies:
        copy.start()
    after = after_in_a("gx")
    for p in range(pieces):
        copies[p].wait()
        for t in range(p * rows // pieces // 8, (p + 1) * rows // pieces // 8):
            for j in range(WIDTH):
                low = field_here[pl.ds(t * 8 * x_size + j, 8, stride=x_size), :]
                high = field_here[pl.ds(t * 8 * x_size + x_size - WIDTH + j, 8, stride=x_size), :]
                to_a[j * rows + t * 8 : j * rows + t * 8 + 8, :] = jnp.where(after, high, low)
                to_b[j * rows + t * 8 : j * rows + t * 8 + 8, :] = jnp.where(after, low, high)
    copies[pieces].wait()
    for t in range(levels // 8):
        low = wind_here[pl.ds(t * 8 * x_size, 8, stride=x_size), :]
        high = wind_here[pl.ds(t * 8 * x_size + x_size - 1, 8, stride=x_size), :]
        at = WIDTH * rows + t * 8
        to_a[at : at + 8, :] = jnp.where(after, high, low)
        to_b[at : at + 8, :] = jnp.where(after, low, high)


def extract_kernel(x_size, chunk, with_wind, field, *refs):
    if with_wind:
        wind, packed = refs
    else:
        to_a, to_b, packed = refs
    rows = packed.shape[0]
    if with_wind:
        levels = wind.shape[0] // (2 * x_size)
        rows = rows - levels
    after = after_in_a("gx")

    def one(t, carry):
        base = pl.multiple_of((chunk * rows + t * 8) * x_size, 8 * x_size)
        edges = None
        for x in range(x_size):
            edges = pack_edges(edges, field[pl.ds(base + x, 8, stride=x_size), :], x)
        packed[pl.ds(pl.multiple_of(t * 8, 8), 8), :] = edges
        if not with_wind:
            for j in range(WIDTH):
                low = field[pl.ds(base + j, 8, stride=x_size), :]
                high = field[pl.ds(base + x_size - WIDTH + j, 8, stride=x_size), :]
                at = pl.ds(pl.multiple_of(j * rows + t * 8, 8), 8)
                to_a[at, :] = jnp.where(after, high, low)
                to_b[at, :] = jnp.where(after, low, high)
        return carry

    lax.fori_loop(0, rows // 8, one, 0, unroll=4)
    if with_wind:

        def one_wind(t, carry):
            base = pl.multiple_of((levels + t * 8) * x_size, 8 * x_size)
            edges = None
            for x in range(x_size):
                edges = pack_edges(edges, wind[pl.ds(base + x, 8, stride=x_size), :], x)
            packed[pl.ds(pl.multiple_of(rows + t * 8, 8), 8), :] = edges
            return carry

        lax.fori_loop(0, levels // 8, one_wind, 0, unroll=4)


def join_packs(after, from_a, from_b):
    south = jnp.where(after, from_b, from_a)
    north = jnp.where(after, from_a, from_b)
    return jnp.where((lane_index(south.shape) & (GROUP - 1)) < WIDTH, south, north)


def wind_kernel(x_size, rows, wind, factor, pack_a, pack_b, *outs):
    speed_x, ahead_y, behind_y, edge_ahead, edge_behind, scales = outs
    levels = speed_x.shape[1]
    after_y = after_in_a("gy")
    for x in range(x_size):
        mapped = factor[pl.ds(x, 1), :]
        for k, divisor in enumerate(DIVISORS):
            scales[k, x] = jnp.broadcast_to(mapped * mapped * (-1.0 / divisor), scales.shape[2:])

    def one(t, carry):
        base = pl.multiple_of(t * 8 * x_size, 8 * x_size)
        at = pl.ds(pl.multiple_of(t * 8, 8), 8)
        before = jnp.zeros((8, wind.shape[1]), jnp.float32)
        for x in range(x_size + 1):
            now = jnp.zeros_like(before) if x == x_size else wind[pl.ds(base + x, 8, stride=x_size), :]
            speed_x[x, at, :] = face_scale * (before + now)
            before = now
        base = base + levels * x_size
        lane = lane_index(before.shape)
        there = pl.ds(pl.multiple_of(rows + t * 8, 8), 8)
        halo = join_packs(after_y, pack_a[there, :], pack_b[there, :])
        forward, backward = None, None
        for x in range(x_size):
            row = wind[pl.ds(base + x, 8, stride=x_size), :]
            edge = rolled(halo, -(GROUP * x + WIDTH))
            front = face_scale * (row + ahead(row, edge, lane, 1))
            back = face_scale * (row + ahead(row, edge, lane, -1))
            ahead_y[x, at, :] = front
            behind_y[x, at, :] = back
            forward = pack_edges(forward, front, x)
            backward = pack_edges(backward, back, x)
        edge_ahead[at, :] = forward
        edge_behind[at, :] = backward
        return carry

    lax.fori_loop(0, levels // 8, one, 0, unroll=UNROLL)


def stencil_matrices(y_size):
    inner = np.zeros((y_size, 4 * y_size), np.float32)
    edges = np.zeros((y_size, 4 * y_size), np.float32)
    for part, (taps, offset) in enumerate(((HIGH, -2), (DAMP, -2), (HIGH, -3), (DAMP, -3))):
        for n, tap in enumerate(taps):
            k = n + offset
            for j in range(y_size):
                if 0 <= j + k < y_size:
                    inner[j + k, part * y_size + j] = tap
            for g in range(0, y_size, GROUP):
                for j in range(WIDTH):
                    if j + k < 0:
                        edges[g + WIDTH + j + k, part * y_size + g + WIDTH + j] = tap
                    if j - WIDTH + k >= 0:
                        edges[g + j + k, part * y_size + g + j] = tap
    return [jnp.asarray(np.concatenate([m, m]).astype(ml_dtypes.bfloat16)) for m in (inner, edges)]


def split_halves(values):
    leading = values.astype(jnp.bfloat16)
    trailing = (values - leading.astype(jnp.float32)).astype(jnp.bfloat16)
    return jnp.concatenate([leading, trailing], axis=1)


def stencil_product(halves, matrix, columns=slice(None)):
    return jnp.dot(halves, matrix[:, columns], preferred_element_type=jnp.float32)


def section_kernel(x_size, k, chunk, last, with_city, *refs):
    refs = list(refs)
    first = k == 0
    section = refs.pop(0)
    base_ref = section if first else refs.pop(0)
    from_a, from_b, pack_a, pack_b = [refs.pop(0) for _ in range(4)]
    wind_a, wind_b = [refs.pop(0) for _ in range(2)]
    speed_x, ahead_y, behind_y, edge_ahead, edge_behind, scales = [refs.pop(0) for _ in range(6)]
    inner_matrix, edge_matrix = [refs.pop(0) for _ in range(2)]
    parts = refs[-4:]
    share = refs[-5]
    refs = refs[:-5]
    if last:
        if with_city:
            city = [refs.pop(0) for _ in range(6)]
            out, wall_out, indoor_out = refs
        else:
            refs.pop(0)
            (out,) = refs
    else:
        out, to_a, to_b, packed = refs
    levels, y_size = edge_ahead.shape
    chunk_rows = base_ref.shape[0] // (CHUNKS * x_size)
    after_x, after_y = after_in_a("gx"), after_in_a("gy")

    def block(g, carry):
        corner = pl.multiple_of((chunk * chunk_rows + g * levels) * x_size, levels * x_size)
        here = pl.multiple_of(g * levels, levels)
        for p in range(levels * x_size // PIECE):
            n = PIECE // levels
            if first:
                lines = [section[pl.ds(corner + x, levels, stride=x_size), :] for x in range(p * n, (p + 1) * n)]
                values = jnp.concatenate(lines, axis=0)
            else:
                values = section[p * n : (p + 1) * n, pl.ds(here, levels), :].reshape(PIECE, y_size)
            halves = split_halves(values)
            for pair in range(2):
                product = stencil_product(halves, inner_matrix, slice(2 * pair * y_size, 2 * (pair + 1) * y_size))
                for j, part in enumerate(parts[2 * pair : 2 * pair + 2]):
                    part[p * PIECE : (p + 1) * PIECE, :] = product[:, j * y_size : (j + 1) * y_size]
        halo = join_packs(after_y, pack_a[pl.ds(here, levels), :], pack_b[pl.ds(here, levels), :])
        product = stencil_product(split_halves(halo), edge_matrix)
        after, before = edge_ahead[...], edge_behind[...]
        share[...] = (
            after * product[:, :y_size]
            - jnp.abs(after) * product[:, y_size : 2 * y_size]
            - before * product[:, 2 * y_size : 3 * y_size]
            + jnp.abs(before) * product[:, 3 * y_size :]
        )

        def one(t, carry):
            at = pl.ds(pl.multiple_of(t * 8, 8), 8)
            rows_at = pl.ds(pl.multiple_of(here + t * 8, 8), 8)
            start = pl.multiple_of(corner + t * 8 * x_size, 8 * x_size)

            def halo_rows(mine, other, j):
                edge_at = pl.ds(pl.multiple_of(j * chunk_rows + here + t * 8, 8), 8)
                return jnp.where(after_x, mine[edge_at, :], other[edge_at, :])

            def outer_wind(mine, other):
                wind_at = pl.ds(pl.multiple_of(WIDTH * chunk_rows + t * 8, 8), 8)
                return jnp.where(after_x, mine[wind_at, :], other[wind_at, :])

            def cell(x):
                if x < 0:
                    return halo_rows(from_b, from_a, x + WIDTH)
                if x >= x_size:
                    return halo_rows(from_a, from_b, x - x_size)
                return section[pl.ds(start + x, 8, stride=x_size), :] if first else section[x, rows_at, :]

            lane = lane_index((8, y_size))
            edge_lane = (lane < WIDTH) | (lane >= y_size - WIDTH)
            edge_share = share[at, :]
            q = [cell(x) for x in range(-3, 2)]
            d1 = [q[i + 1] - q[i] for i in range(4)]
            d2 = [d1[i + 1] - d1[i] for i in range(3)]
            d3 = [d2[i + 1] - d2[i] for i in range(2)]
            d4 = d3[1] - d3[0]
            smooth = d4 - 5.0 * d2[1] + 30.0 * q[2]
            q, d1, d2, d3 = q[3:], d1[-1], d2[-1], d3[-1]
            flux_before = None
            edges, lows = None, []
            for x in range(-1, x_size):
                q.append(cell(x + WIDTH))
                new1 = q[-1] - q[-2]
                new2 = new1 - d1
                new3 = new2 - d2
                new4 = new3 - d3
                new_smooth = new4 - 5.0 * d2 + 30.0 * q[0]
                speed = speed_x[x + 1, at, :]
                if x == -1:
                    speed = speed + face_scale * outer_wind(wind_b, wind_a)
                if x == x_size - 1:
                    speed = speed + face_scale * outer_wind(wind_a, wind_b)
                flux = speed * (smooth + new_smooth) - jnp.abs(speed) * (new4 - d4)
                d1, d2, d3, d4, smooth = new1, new2, new3, new4, new_smooth
                if x >= 0:
                    lines = [part[pl.ds(pl.multiple_of(x * levels + t * 8, 8), 8), :] for part in parts]
                    after, before = ahead_y[x, at, :], behind_y[x, at, :]
                    moved = rolled(edge_share, -(GROUP * x + WIDTH))
                    divergence = (
                        (flux - flux_before)
                        + (after * lines[0] - jnp.abs(after) * lines[1])
                        - (before * lines[2] - jnp.abs(before) * lines[3])
                        + jnp.where(edge_lane, moved, 0.0)
                    )
                    base = base_ref[pl.ds(start + x, 8, stride=x_size), :]
                    new = base + scales[k, x] * divergence
                    if last:
                        out[pl.ds(pl.multiple_of(t * 8 * x_size, 8 * x_size) + x, 8, stride=x_size), :] = new
                    else:
                        out[x, rows_at, :] = new
                        edges = pack_edges(edges, new, x)
                        if x < WIDTH:
                            lows.append(new)
                        if x >= x_size - WIDTH:
                            j = x - x_size + WIDTH
                            edge_at = pl.ds(pl.multiple_of(j * chunk_rows + here + t * 8, 8), 8)
                            to_a[edge_at, :] = jnp.where(after_x, new, lows[j])
                            to_b[edge_at, :] = jnp.where(after_x, lows[j], new)
                flux_before = flux
                q = q[1:]
            if not last:
                packed[rows_at, :] = edges
            return carry

        lax.fori_loop(0, levels // 8, one, 0, unroll=UNROLL)
        return carry

    if last:
        block(pl.program_id(0), 0)
    else:
        lax.fori_loop(0, chunk_rows // levels, block, 0)
    if last and with_city:

        @pl.when(pl.program_id(0) == 0)
        def _():
            city_step(x_size, out, *city, wall_out, indoor_out)


def dot(a, b, dims):
    return lax.dot_general(
        a, b, (dims, ((), ())), precision=lax.Precision.HIGHEST, preferred_element_type=jnp.float32
    )


def city_step(x_size, out, counts, cols_ref, class_ref, table, wall_ref, indoor_ref, wall_out, indoor_out):
    deep = 16
    cols = cols_ref[...]
    slots = cols.shape[1]
    y_size = out.shape[1]
    cell_x = lax.div(cols, y_size)
    cell_y = lax.rem(cols, y_size)
    lower = [
        jnp.concatenate([out[pl.ds(8 * x_size * t + x, 8, stride=x_size), :] for t in range(deep // 8)], axis=0)
        for x in range(x_size)
    ]
    at_y = (lax.broadcasted_iota(jnp.int32, (y_size, slots), 0) == cell_y).astype(jnp.float32)
    gathered = dot(jnp.concatenate(lower, axis=0), at_y, ((1,), (0,)))
    air = jnp.zeros((deep, slots), jnp.float32)
    for x in range(x_size):
        air = jnp.where(cell_x == x, gathered[deep * x : deep * (x + 1)], air)
    air = air[:UL]
    onehot = (lax.broadcasted_iota(jnp.int32, (NCLS, slots), 0) == class_ref[...]).astype(jnp.float32)
    areas = dot(table[...], onehot, ((0,), (0,)))
    walls = wall_ref[...]
    indoor = indoor_ref[...]
    heat = heat_coef * areas * (walls[0:1] - air)
    wall_first = walls[0:1] - wall_coef * jnp.sum(heat, axis=0, keepdims=True) + conduct * (walls[1:2] - walls[0:1])
    middle = walls[1:-1] + conduct * (walls[:-2] - 2.0 * walls[1:-1] + walls[2:])
    last = walls[-1:] + conduct * (walls[-2:-1] - walls[-1:]) + inner_coef * (indoor - walls[-1:])
    indoor_new = indoor + room_coef * (walls[-1:] - indoor)
    live = lax.broadcasted_iota(jnp.int32, (1, slots), 1) < counts[0]
    wall_out[...] = jnp.where(live, jnp.concatenate([wall_first, middle, last], axis=0), walls)
    indoor_out[...] = jnp.where(live, indoor_new, indoor)
    heating = jnp.where(live, flux_coef * heat, 0.0)
    heating = jnp.concatenate([heating, jnp.zeros((deep - UL, slots), jnp.float32)], axis=0)
    spread = jnp.concatenate([jnp.where(cell_x == x, heating, 0.0) for x in range(x_size)], axis=0)
    added = dot(spread, at_y, ((1,), (1,)))
    for x in range(x_size):
        for t in range(deep // 8):
            out[pl.ds(8 * x_size * t + x, 8, stride=x_size), :] = (
                lower[x][8 * t : 8 * t + 8] + added[deep * x + 8 * t : deep * x + 8 * t + 8]
            )


def exchange(axis, to_a, to_b):
    size = lax.axis_size(axis)
    first = AFTER_FIRST[axis]
    pairs = [[(i, (i + 1) % size) for i in range(start, size, 2)] for start in (first, 1 - first)]
    both = [half + [(j, i) for i, j in half] for half in pairs]
    return lax.ppermute(to_a, axis, both[0]), lax.ppermute(to_b, axis, both[1])


def per_device(
    scalars,
    winds,
    map_factor,
    urban_counts,
    urban_cols,
    street_class,
    area_table,
    wall_temp,
    indoor_temp,
):
    n_scalars, levels, x_size, y_size = scalars.shape
    slots = urban_cols.shape[0]
    rows = n_scalars * levels // CHUNKS
    f32 = functools.partial(jax.ShapeDtypeStruct, dtype=jnp.float32)
    field = scalars.reshape(n_scalars * levels * x_size, y_size)
    wind = winds.reshape(2 * levels * x_size, y_size)
    params = pltpu.CompilerParams(vmem_limit_bytes=40 * 2**20)
    whole = pl.BlockSpec(memory_space=pltpu.VMEM)

    smem = pl.BlockSpec(memory_space=pltpu.SMEM)
    hbm = pl.BlockSpec(memory_space=pltpu.HBM)
    cheap = pl.CostEstimate(flops=1000, bytes_accessed=1000, transcendentals=0)

    pieces = 4
    first_rows = pl.pallas_call(
        functools.partial(first_rows_kernel, x_size, rows, levels, pieces),
        in_specs=[hbm, hbm],
        out_specs=[whole] * 2,
        out_shape=[f32((WIDTH * rows + levels, y_size))] * 2,
        scratch_shapes=[
            pltpu.VMEM((rows * x_size, y_size), jnp.float32),
            pltpu.VMEM((levels * x_size, y_size), jnp.float32),
            pltpu.SemaphoreType.DMA((pieces + 1,)),
        ],
        compiler_params=pltpu.CompilerParams(vmem_limit_bytes=62 * 2**20),
        cost_estimate=cheap,
        name="first_rows",
    )(field, wind)
    received = [None] * CHUNKS
    received[0] = exchange("gx", *first_rows)
    for c in range(CHUNKS):
        extra = levels if c == 0 else 0
        outs = pl.pallas_call(
            functools.partial(extract_kernel, x_size, c, c == 0),
            in_specs=[whole] + [whole] * (c == 0),
            out_specs=[whole] * (1 if c == 0 else 3),
            out_shape=[f32((WIDTH * rows, y_size))] * (0 if c == 0 else 2) + [f32((rows + extra, y_size))],
            compiler_params=params,
            cost_estimate=cheap,
            name=f"extract_{c}",
        )(field, *([wind] if c == 0 else []))
        if c > 0:
            received[c] = exchange("gx", *outs[:2])
        received[c] = (*received[c], *exchange("gy", outs[-1], outs[-1]))

    speeds = pl.pallas_call(
        functools.partial(wind_kernel, x_size, rows),
        in_specs=[whole] * 4,
        out_specs=[whole] * 6,
        out_shape=[
            f32((x_size + 1, levels, y_size)),
            f32((x_size, levels, y_size)),
            f32((x_size, levels, y_size)),
            f32((levels, y_size)),
            f32((levels, y_size)),
            f32((len(DIVISORS), x_size, 8, y_size)),
        ],
        compiler_params=params,
        cost_estimate=cheap,
        name="speeds",
    )(wind, map_factor, *received[0][2:])
    winds_beyond = received[0][:2]
    matrices = stencil_matrices(y_size)

    steps = rows // levels
    sections = [None] * CHUNKS
    result = None
    for k in range(len(DIVISORS)):
        last = k == len(DIVISORS) - 1
        for c in range(CHUNKS):
            operands = [field] if k == 0 else [sections[c], field]
            operands += [*received[c], *winds_beyond, *speeds, *matrices]
            specs = [whole] * len(operands)
            city = last and c == 0
            aliases = {}
            flat_c = pl.BlockSpec((levels * x_size, y_size), lambda g, c=c: (c * steps + g, 0))
            if city:
                operands += [
                    urban_counts,
                    urban_cols[None],
                    street_class[None],
                    area_table,
                    wall_temp,
                    indoor_temp[None],
                ]
                specs += [smem] + [whole] * 5
                out_specs = [flat_c, whole, whole]
                out_shape = [f32(field.shape), f32(wall_temp.shape), f32((1, slots))]
            elif last:
                aliases = {len(operands): 0}
                operands += [result]
                specs += [pl.BlockSpec(memory_space=pl.ANY)]
                out_specs = [flat_c]
                out_shape = [f32(field.shape)]
            else:
                out_specs = [whole] * 4
                out_shape = [
                    f32((x_size, rows, y_size)),
                    f32((WIDTH * rows, y_size)),
                    f32((WIDTH * rows, y_size)),
                    f32((rows, y_size)),
                ]
            outs = pl.pallas_call(
                functools.partial(section_kernel, x_size, k, c, last, city),
                grid=(steps,) if last else (),
                in_specs=specs,
                out_specs=out_specs,
                out_shape=out_shape,
                scratch_shapes=[pltpu.VMEM((levels, y_size), jnp.float32)]
                + [pltpu.VMEM((levels * x_size, y_size), jnp.float32)] * 4,
                input_output_aliases=aliases,
                compiler_params=params,
                cost_estimate=cheap,
                name=f"section_{k}_{c}",
            )(*operands)
            if city:
                result, wall_out, indoor_out = outs
            elif last:
                (result,) = outs
            else:
                sections[c], *outgoing, packed = outs
                received[c] = (*exchange("gx", *outgoing), *exchange("gy", packed, packed))
    return (result.reshape(scalars.shape), wall_out, indoor_out[0])


def solution(mesh):
    in_specs = (
        P(None, None, "gx", "gy"),
        P(None, None, "gx", "gy"),
        P("gx", "gy"),
        P(("gx", "gy")),
        P(("gx", "gy")),
        P(("gx", "gy")),
        P(),
        P(None, ("gx", "gy")),
        P(("gx", "gy")),
    )
    out_specs = (P(None, None, "gx", "gy"), P(None, ("gx", "gy")), P(("gx", "gy")))
    return jax.shard_map(
        per_device, mesh=mesh, in_specs=in_specs, out_specs=out_specs, check_vma=False
    )
```

```python
import functools

import jax
import jax.numpy as jnp
import ml_dtypes
import numpy as np
from jax import lax
from jax.experimental import pallas as pl
from jax.experimental.pallas import tpu as pltpu
from jax.sharding import PartitionSpec as P

UL = 10
NWL = 10
NCLS = 10
WIDTH = 3
GROUP = 8
CHUNKS = 2
PIECE = 512
UNROLL = 2
DIVISORS = (3.0, 2.0, 1.0)
HIGH = (1, -8, 37, 37, -8, 1)
DAMP = (-1, 5, -10, 10, -5, 1)

heat_coef = 0.5
wall_coef = 0.05
conduct = 0.3
inner_coef = 0.2
room_coef = 0.1
flux_coef = 0.5
face_scale = 0.5 / 60.0


def lane_index(shape):
    return lax.broadcasted_iota(jnp.int32, shape, 1)


def rolled(array, shift):
    return pltpu.roll(array, shift % array.shape[1], 1)


def pack_edges(packed, row, x):
    moved = rolled(row, GROUP * x + WIDTH)
    lane = lane_index(row.shape)
    here = (lane >= GROUP * x) & (lane < GROUP * x + 2 * WIDTH)
    return moved if packed is None else jnp.where(here, moved, packed)


def ahead(row, halo, lane, k):
    if k > 0:
        return rolled(jnp.where(lane < k, halo, row), -k)
    return rolled(jnp.where(lane >= row.shape[1] + k, halo, row), -k)


def even_index(axis):
    return lax.rem(lax.axis_index(axis), 2) == 0


def first_rows_kernel(x_size, rows, levels, pieces, field, wind, to_a, to_b, field_here, wind_here, sems):
    size = rows * x_size // pieces
    copies = [
        pltpu.make_async_copy(field.at[pl.ds(p * size, size), :], field_here.at[pl.ds(p * size, size), :], sems.at[p])
        for p in range(pieces)
    ]
    copies.append(pltpu.make_async_copy(wind.at[pl.ds(0, levels * x_size), :], wind_here, sems.at[pieces]))
    for copy in copies:
        copy.start()
    even = even_index("gx")
    for p in range(pieces):
        copies[p].wait()
        for t in range(p * rows // pieces // 8, (p + 1) * rows // pieces // 8):
            for j in range(WIDTH):
                low = field_here[pl.ds(t * 8 * x_size + j, 8, stride=x_size), :]
                high = field_here[pl.ds(t * 8 * x_size + x_size - WIDTH + j, 8, stride=x_size), :]
                to_a[j * rows + t * 8 : j * rows + t * 8 + 8, :] = jnp.where(even, high, low)
                to_b[j * rows + t * 8 : j * rows + t * 8 + 8, :] = jnp.where(even, low, high)
    copies[pieces].wait()
    for t in range(levels // 8):
        low = wind_here[pl.ds(t * 8 * x_size, 8, stride=x_size), :]
        high = wind_here[pl.ds(t * 8 * x_size + x_size - 1, 8, stride=x_size), :]
        at = WIDTH * rows + t * 8
        to_a[at : at + 8, :] = jnp.where(even, high, low)
        to_b[at : at + 8, :] = jnp.where(even, low, high)


def extract_kernel(x_size, chunk, with_wind, field, *refs):
    if with_wind:
        wind, packed = refs
    else:
        to_a, to_b, packed = refs
    rows = packed.shape[0]
    if with_wind:
        levels = wind.shape[0] // (2 * x_size)
        rows = rows - levels
    even = even_index("gx")

    def one(t, carry):
        base = pl.multiple_of((chunk * rows + t * 8) * x_size, 8 * x_size)
        edges = None
        for x in range(x_size):
            edges = pack_edges(edges, field[pl.ds(base + x, 8, stride=x_size), :], x)
        packed[pl.ds(pl.multiple_of(t * 8, 8), 8), :] = edges
        if not with_wind:
            for j in range(WIDTH):
                low = field[pl.ds(base + j, 8, stride=x_size), :]
                high = field[pl.ds(base + x_size - WIDTH + j, 8, stride=x_size), :]
                at = pl.ds(pl.multiple_of(j * rows + t * 8, 8), 8)
                to_a[at, :] = jnp.where(even, high, low)
                to_b[at, :] = jnp.where(even, low, high)
        return carry

    lax.fori_loop(0, rows // 8, one, 0, unroll=4)
    if with_wind:

        def one_wind(t, carry):
            base = pl.multiple_of((levels + t * 8) * x_size, 8 * x_size)
            edges = None
            for x in range(x_size):
                edges = pack_edges(edges, wind[pl.ds(base + x, 8, stride=x_size), :], x)
            packed[pl.ds(pl.multiple_of(rows + t * 8, 8), 8), :] = edges
            return carry

        lax.fori_loop(0, levels // 8, one_wind, 0, unroll=4)


def join_packs(even, from_a, from_b):
    south = jnp.where(even, from_b, from_a)
    north = jnp.where(even, from_a, from_b)
    return jnp.where((lane_index(south.shape) & (GROUP - 1)) < WIDTH, south, north)


def wind_kernel(x_size, rows, wind, factor, pack_a, pack_b, *outs):
    speed_x, ahead_y, behind_y, edge_ahead, edge_behind, scales = outs
    levels = speed_x.shape[1]
    even_y = even_index("gy")
    for x in range(x_size):
        mapped = factor[pl.ds(x, 1), :]
        for k, divisor in enumerate(DIVISORS):
            scales[k, x] = jnp.broadcast_to(mapped * mapped * (-1.0 / divisor), scales.shape[2:])

    def one(t, carry):
        base = pl.multiple_of(t * 8 * x_size, 8 * x_size)
        at = pl.ds(pl.multiple_of(t * 8, 8), 8)
        before = jnp.zeros((8, wind.shape[1]), jnp.float32)
        for x in range(x_size + 1):
            now = jnp.zeros_like(before) if x == x_size else wind[pl.ds(base + x, 8, stride=x_size), :]
            speed_x[x, at, :] = face_scale * (before + now)
            before = now
        base = base + levels * x_size
        lane = lane_index(before.shape)
        there = pl.ds(pl.multiple_of(rows + t * 8, 8), 8)
        halo = join_packs(even_y, pack_a[there, :], pack_b[there, :])
        forward, backward = None, None
        for x in range(x_size):
            row = wind[pl.ds(base + x, 8, stride=x_size), :]
            edge = rolled(halo, -(GROUP * x + WIDTH))
            front = face_scale * (row + ahead(row, edge, lane, 1))
            back = face_scale * (row + ahead(row, edge, lane, -1))
            ahead_y[x, at, :] = front
            behind_y[x, at, :] = back
            forward = pack_edges(forward, front, x)
            backward = pack_edges(backward, back, x)
        edge_ahead[at, :] = forward
        edge_behind[at, :] = backward
        return carry

    lax.fori_loop(0, levels // 8, one, 0, unroll=UNROLL)


def stencil_matrices(y_size):
    inner = np.zeros((y_size, 4 * y_size), np.float32)
    edges = np.zeros((y_size, 4 * y_size), np.float32)
    for part, (taps, offset) in enumerate(((HIGH, -2), (DAMP, -2), (HIGH, -3), (DAMP, -3))):
        for n, tap in enumerate(taps):
            k = n + offset
            for j in range(y_size):
                if 0 <= j + k < y_size:
                    inner[j + k, part * y_size + j] = tap
            for g in range(0, y_size, GROUP):
                for j in range(WIDTH):
                    if j + k < 0:
                        edges[g + WIDTH + j + k, part * y_size + g + WIDTH + j] = tap
                    if j - WIDTH + k >= 0:
                        edges[g + j + k, part * y_size + g + j] = tap
    return [jnp.asarray(np.concatenate([m, m]).astype(ml_dtypes.bfloat16)) for m in (inner, edges)]


def split_halves(values):
    leading = values.astype(jnp.bfloat16)
    trailing = (values - leading.astype(jnp.float32)).astype(jnp.bfloat16)
    return jnp.concatenate([leading, trailing], axis=1)


def stencil_product(halves, matrix, columns=slice(None)):
    return jnp.dot(halves, matrix[:, columns], preferred_element_type=jnp.float32)


def linear_parts(
    x_size, first, section, corner, here, levels, pack_a, pack_b, after_y, edge_ahead, edge_behind,
    inner_matrix, edge_matrix, share, parts,
):
    y_size = section.shape[-1]
    for p in range(levels * x_size // PIECE):
        n = PIECE // levels
        if first:
            lines = [section[pl.ds(corner + x, levels, stride=x_size), :] for x in range(p * n, (p + 1) * n)]
            values = jnp.concatenate(lines, axis=0)
        else:
            values = section[p * n : (p + 1) * n, pl.ds(here, levels), :].reshape(PIECE, y_size)
        halves = split_halves(values)
        for pair in range(2):
            product = stencil_product(halves, inner_matrix, slice(2 * pair * y_size, 2 * (pair + 1) * y_size))
            for j, part in enumerate(parts[2 * pair : 2 * pair + 2]):
                part[p * PIECE : (p + 1) * PIECE, :] = product[:, j * y_size : (j + 1) * y_size]
    halo = join_packs(after_y, pack_a[pl.ds(here, levels), :], pack_b[pl.ds(here, levels), :])
    product = stencil_product(split_halves(halo), edge_matrix)
    after, before = edge_ahead[...], edge_behind[...]
    share[...] = (
        after * product[:, :y_size]
        - jnp.abs(after) * product[:, y_size : 2 * y_size]
        - before * product[:, 2 * y_size : 3 * y_size]
        + jnp.abs(before) * product[:, 3 * y_size :]
    )


def south_north(x, at, edge_share, edge_lane, levels, ahead_y, behind_y, parts):
    lines = [part[pl.ds(pl.multiple_of(x * levels, levels) + at.start, 8), :] for part in parts]
    after, before = ahead_y[x, at, :], behind_y[x, at, :]
    moved = rolled(edge_share, -(GROUP * x + WIDTH))
    return (
        (after * lines[0] - jnp.abs(after) * lines[1])
        - (before * lines[2] - jnp.abs(before) * lines[3])
        + jnp.where(edge_lane, moved, 0.0)
    )


def south_north_kernel(
    section, pack_a, pack_b, ahead_y, behind_y, edge_ahead, edge_behind, inner_matrix, edge_matrix, out, share, *parts
):
    x_size, chunk_rows, y_size = section.shape
    levels = edge_ahead.shape[0]
    after_y = even_index("gy")

    def block(g, carry):
        here = pl.multiple_of(g * levels, levels)
        linear_parts(
            x_size, False, section, None, here, levels, pack_a, pack_b, after_y, edge_ahead, edge_behind,
            inner_matrix, edge_matrix, share, parts,
        )

        def one(t, carry):
            at = pl.ds(pl.multiple_of(t * 8, 8), 8)
            lane = lane_index((8, y_size))
            edge_lane = (lane < WIDTH) | (lane >= y_size - WIDTH)
            edge_share = share[at, :]
            for x in range(x_size):
                out[x, pl.ds(pl.multiple_of(here + t * 8, 8), 8), :] = south_north(
                    x, at, edge_share, edge_lane, levels, ahead_y, behind_y, parts
                )
            return carry

        lax.fori_loop(0, levels // 8, one, 0, unroll=UNROLL)
        return carry

    lax.fori_loop(0, chunk_rows // levels, block, 0)


def section_kernel(x_size, k, chunk, last, with_city, split, *refs):
    refs = list(refs)
    first = k == 0
    section = refs.pop(0)
    base_ref = section if first else refs.pop(0)
    from_a, from_b, pack_a, pack_b = [refs.pop(0) for _ in range(4)]
    wind_a, wind_b = [refs.pop(0) for _ in range(2)]
    speed_x, ahead_y, behind_y, edge_ahead, edge_behind, scales = [refs.pop(0) for _ in range(6)]
    inner_matrix, edge_matrix = [refs.pop(0) for _ in range(2)]
    if split:
        turned = refs.pop(0)
    else:
        parts = refs[-4:]
        share = refs[-5]
        refs = refs[:-5]
    if last:
        if with_city:
            city = [refs.pop(0) for _ in range(6)]
            out, wall_out, indoor_out = refs
        else:
            refs.pop(0)
            (out,) = refs
    else:
        out, to_a, to_b, packed = refs
    levels, y_size = edge_ahead.shape
    chunk_rows = base_ref.shape[0] // (CHUNKS * x_size)
    even_x, after_y = even_index("gx"), even_index("gy")

    def block(g, carry):
        corner = pl.multiple_of((chunk * chunk_rows + g * levels) * x_size, levels * x_size)
        here = pl.multiple_of(g * levels, levels)
        if not split:
            linear_parts(
                x_size, first, section, corner, here, levels, pack_a, pack_b, after_y, edge_ahead, edge_behind,
                inner_matrix, edge_matrix, share, parts,
            )

        def one(t, carry):
            at = pl.ds(pl.multiple_of(t * 8, 8), 8)
            rows_at = pl.ds(pl.multiple_of(here + t * 8, 8), 8)
            start = pl.multiple_of(corner + t * 8 * x_size, 8 * x_size)

            def halo_rows(mine, other, j):
                edge_at = pl.ds(pl.multiple_of(j * chunk_rows + here + t * 8, 8), 8)
                return jnp.where(even_x, mine[edge_at, :], other[edge_at, :])

            def outer_wind(mine, other):
                wind_at = pl.ds(pl.multiple_of(WIDTH * chunk_rows + t * 8, 8), 8)
                return jnp.where(even_x, mine[wind_at, :], other[wind_at, :])

            def cell(x):
                if x < 0:
                    return halo_rows(from_b, from_a, x + WIDTH)
                if x >= x_size:
                    return halo_rows(from_a, from_b, x - x_size)
                return section[pl.ds(start + x, 8, stride=x_size), :] if first else section[x, rows_at, :]

            lane = lane_index((8, y_size))
            edge_lane = (lane < WIDTH) | (lane >= y_size - WIDTH)
            edge_share = None if split else share[at, :]
            q = [cell(x) for x in range(-3, 2)]
            d1 = [q[i + 1] - q[i] for i in range(4)]
            d2 = [d1[i + 1] - d1[i] for i in range(3)]
            d3 = [d2[i + 1] - d2[i] for i in range(2)]
            d4 = d3[1] - d3[0]
            smooth = d4 - 5.0 * d2[1] + 30.0 * q[2]
            q, d1, d2, d3 = q[3:], d1[-1], d2[-1], d3[-1]
            flux_before = None
            edges, lows = None, []
            for x in range(-1, x_size):
                q.append(cell(x + WIDTH))
                new1 = q[-1] - q[-2]
                new2 = new1 - d1
                new3 = new2 - d2
                new4 = new3 - d3
                new_smooth = new4 - 5.0 * d2 + 30.0 * q[0]
                speed = speed_x[x + 1, at, :]
                if x == -1:
                    speed = speed + face_scale * outer_wind(wind_b, wind_a)
                if x == x_size - 1:
                    speed = speed + face_scale * outer_wind(wind_a, wind_b)
                flux = speed * (smooth + new_smooth) - jnp.abs(speed) * (new4 - d4)
                d1, d2, d3, d4, smooth = new1, new2, new3, new4, new_smooth
                if x >= 0:
                    if split:
                        turn = turned[x, rows_at, :]
                    else:
                        turn = south_north(x, at, edge_share, edge_lane, levels, ahead_y, behind_y, parts)
                    divergence = (flux - flux_before) + turn
                    base = base_ref[pl.ds(start + x, 8, stride=x_size), :]
                    new = base + scales[k, x] * divergence
                    if last:
                        out[pl.ds(pl.multiple_of(t * 8 * x_size, 8 * x_size) + x, 8, stride=x_size), :] = new
                    else:
                        out[x, rows_at, :] = new
                        edges = pack_edges(edges, new, x)
                        if x < WIDTH:
                            lows.append(new)
                        if x >= x_size - WIDTH:
                            j = x - x_size + WIDTH
                            edge_at = pl.ds(pl.multiple_of(j * chunk_rows + here + t * 8, 8), 8)
                            to_a[edge_at, :] = jnp.where(even_x, new, lows[j])
                            to_b[edge_at, :] = jnp.where(even_x, lows[j], new)
                flux_before = flux
                q = q[1:]
            if not last:
                packed[rows_at, :] = edges
            return carry

        lax.fori_loop(0, levels // 8, one, 0, unroll=UNROLL)
        return carry

    if last:
        block(pl.program_id(0), 0)
    else:
        lax.fori_loop(0, chunk_rows // levels, block, 0)
    if last and with_city:

        @pl.when(pl.program_id(0) == 0)
        def _():
            city_step(x_size, out, *city, wall_out, indoor_out)


def dot(a, b, dims):
    return lax.dot_general(
        a, b, (dims, ((), ())), precision=lax.Precision.HIGHEST, preferred_element_type=jnp.float32
    )


def city_step(x_size, out, counts, cols_ref, class_ref, table, wall_ref, indoor_ref, wall_out, indoor_out):
    deep = 16
    cols = cols_ref[...]
    slots = cols.shape[1]
    y_size = out.shape[1]
    cell_x = lax.div(cols, y_size)
    cell_y = lax.rem(cols, y_size)
    lower = [
        jnp.concatenate([out[pl.ds(8 * x_size * t + x, 8, stride=x_size), :] for t in range(deep // 8)], axis=0)
        for x in range(x_size)
    ]
    at_y = (lax.broadcasted_iota(jnp.int32, (y_size, slots), 0) == cell_y).astype(jnp.float32)
    gathered = dot(jnp.concatenate(lower, axis=0), at_y, ((1,), (0,)))
    air = jnp.zeros((deep, slots), jnp.float32)
    for x in range(x_size):
        air = jnp.where(cell_x == x, gathered[deep * x : deep * (x + 1)], air)
    air = air[:UL]
    onehot = (lax.broadcasted_iota(jnp.int32, (NCLS, slots), 0) == class_ref[...]).astype(jnp.float32)
    areas = dot(table[...], onehot, ((0,), (0,)))
    walls = wall_ref[...]
    indoor = indoor_ref[...]
    heat = heat_coef * areas * (walls[0:1] - air)
    wall_first = walls[0:1] - wall_coef * jnp.sum(heat, axis=0, keepdims=True) + conduct * (walls[1:2] - walls[0:1])
    middle = walls[1:-1] + conduct * (walls[:-2] - 2.0 * walls[1:-1] + walls[2:])
    last = walls[-1:] + conduct * (walls[-2:-1] - walls[-1:]) + inner_coef * (indoor - walls[-1:])
    indoor_new = indoor + room_coef * (walls[-1:] - indoor)
    live = lax.broadcasted_iota(jnp.int32, (1, slots), 1) < counts[0]
    wall_out[...] = jnp.where(live, jnp.concatenate([wall_first, middle, last], axis=0), walls)
    indoor_out[...] = jnp.where(live, indoor_new, indoor)
    heating = jnp.where(live, flux_coef * heat, 0.0)
    heating = jnp.concatenate([heating, jnp.zeros((deep - UL, slots), jnp.float32)], axis=0)
    spread = jnp.concatenate([jnp.where(cell_x == x, heating, 0.0) for x in range(x_size)], axis=0)
    added = dot(spread, at_y, ((1,), (1,)))
    for x in range(x_size):
        for t in range(deep // 8):
            out[pl.ds(8 * x_size * t + x, 8, stride=x_size), :] = (
                lower[x][8 * t : 8 * t + 8] + added[deep * x + 8 * t : deep * x + 8 * t + 8]
            )


def exchange(axis, to_a, to_b):
    size = lax.axis_size(axis)
    pairs_a = [(i, i + 1) for i in range(0, size, 2)]
    pairs_b = [(i, (i + 1) % size) for i in range(1, size, 2)]
    both = [pairs + [(j, i) for i, j in pairs] for pairs in (pairs_a, pairs_b)]
    return lax.ppermute(to_a, axis, both[0]), lax.ppermute(to_b, axis, both[1])


def per_device(
    scalars,
    winds,
    map_factor,
    urban_counts,
    urban_cols,
    street_class,
    area_table,
    wall_temp,
    indoor_temp,
):
    n_scalars, levels, x_size, y_size = scalars.shape
    slots = urban_cols.shape[0]
    rows = n_scalars * levels // CHUNKS
    f32 = functools.partial(jax.ShapeDtypeStruct, dtype=jnp.float32)
    field = scalars.reshape(n_scalars * levels * x_size, y_size)
    wind = winds.reshape(2 * levels * x_size, y_size)
    params = pltpu.CompilerParams(vmem_limit_bytes=40 * 2**20)
    whole = pl.BlockSpec(memory_space=pltpu.VMEM)

    smem = pl.BlockSpec(memory_space=pltpu.SMEM)
    hbm = pl.BlockSpec(memory_space=pltpu.HBM)
    cheap = pl.CostEstimate(flops=1000, bytes_accessed=1000, transcendentals=0)

    pieces = 4
    first_rows = pl.pallas_call(
        functools.partial(first_rows_kernel, x_size, rows, levels, pieces),
        in_specs=[hbm, hbm],
        out_specs=[whole] * 2,
        out_shape=[f32((WIDTH * rows + levels, y_size))] * 2,
        scratch_shapes=[
            pltpu.VMEM((rows * x_size, y_size), jnp.float32),
            pltpu.VMEM((levels * x_size, y_size), jnp.float32),
            pltpu.SemaphoreType.DMA((pieces + 1,)),
        ],
        compiler_params=pltpu.CompilerParams(vmem_limit_bytes=62 * 2**20),
        cost_estimate=cheap,
        name="first_rows",
    )(field, wind)
    received = [None] * CHUNKS
    received[0] = exchange("gx", *first_rows)
    for c in range(CHUNKS):
        extra = levels if c == 0 else 0
        outs = pl.pallas_call(
            functools.partial(extract_kernel, x_size, c, c == 0),
            in_specs=[whole] + [whole] * (c == 0),
            out_specs=[whole] * (1 if c == 0 else 3),
            out_shape=[f32((WIDTH * rows, y_size))] * (0 if c == 0 else 2) + [f32((rows + extra, y_size))],
            compiler_params=params,
            cost_estimate=cheap,
            name=f"extract_{c}",
        )(field, *([wind] if c == 0 else []))
        if c > 0:
            received[c] = exchange("gx", *outs[:2])
        received[c] = (*received[c], *exchange("gy", outs[-1], outs[-1]))

    speeds = pl.pallas_call(
        functools.partial(wind_kernel, x_size, rows),
        in_specs=[whole] * 4,
        out_specs=[whole] * 6,
        out_shape=[
            f32((x_size + 1, levels, y_size)),
            f32((x_size, levels, y_size)),
            f32((x_size, levels, y_size)),
            f32((levels, y_size)),
            f32((levels, y_size)),
            f32((len(DIVISORS), x_size, 8, y_size)),
        ],
        compiler_params=params,
        cost_estimate=cheap,
        name="speeds",
    )(wind, map_factor, *received[0][2:])
    winds_beyond = received[0][:2]
    matrices = stencil_matrices(y_size)

    steps = rows // levels
    sections = [None] * CHUNKS
    result = None
    for k in range(len(DIVISORS)):
        last = k == len(DIVISORS) - 1
        for c in range(CHUNKS):
            operands = [field] if k == 0 else [sections[c], field]
            operands += [*received[c], *winds_beyond, *speeds, *matrices]
            specs = [whole] * len(operands)
            city = last and c == 0
            split = last and c == CHUNKS - 1
            scratch = [pltpu.VMEM((levels, y_size), jnp.float32)]
            scratch += [pltpu.VMEM((levels * x_size, y_size), jnp.float32)] * 4
            if split:
                turned = pl.pallas_call(
                    south_north_kernel,
                    in_specs=[whole] * 9,
                    out_specs=whole,
                    out_shape=f32((x_size, rows, y_size)),
                    scratch_shapes=scratch,
                    compiler_params=params,
                    cost_estimate=cheap,
                    name="south_north",
                )(sections[c], *received[c][2:], *speeds[1:5], *matrices)
                operands += [turned]
                specs += [whole]
                scratch = []
            aliases = {}
            flat_c = pl.BlockSpec((levels * x_size, y_size), lambda g, c=c: (c * steps + g, 0))
            if city:
                operands += [
                    urban_counts,
                    urban_cols[None],
                    street_class[None],
                    area_table,
                    wall_temp,
                    indoor_temp[None],
                ]
                specs += [smem] + [whole] * 5
                out_specs = [flat_c, whole, whole]
                out_shape = [f32(field.shape), f32(wall_temp.shape), f32((1, slots))]
            elif last:
                aliases = {len(operands): 0}
                operands += [result]
                specs += [pl.BlockSpec(memory_space=pl.ANY)]
                out_specs = [flat_c]
                out_shape = [f32(field.shape)]
            else:
                out_specs = [whole] * 4
                out_shape = [
                    f32((x_size, rows, y_size)),
                    f32((WIDTH * rows, y_size)),
                    f32((WIDTH * rows, y_size)),
                    f32((rows, y_size)),
                ]
            outs = pl.pallas_call(
                functools.partial(section_kernel, x_size, k, c, last, city, split),
                grid=(steps,) if last else (),
                in_specs=specs,
                out_specs=out_specs,
                out_shape=out_shape,
                scratch_shapes=scratch,
                input_output_aliases=aliases,
                compiler_params=params,
                cost_estimate=cheap,
                name=f"section_{k}_{c}",
            )(*operands)
            if city:
                result, wall_out, indoor_out = outs
            elif last:
                (result,) = outs
            else:
                sections[c], *outgoing, packed = outs
                received[c] = (*exchange("gx", *outgoing), *exchange("gy", packed, packed))
    return (result.reshape(scalars.shape), wall_out, indoor_out[0])


def solution(mesh):
    in_specs = (
        P(None, None, "gx", "gy"),
        P(None, None, "gx", "gy"),
        P("gx", "gy"),
        P(("gx", "gy")),
        P(("gx", "gy")),
        P(("gx", "gy")),
        P(),
        P(None, ("gx", "gy")),
        P(("gx", "gy")),
    )
    out_specs = (P(None, None, "gx", "gy"), P(None, ("gx", "gy")), P(("gx", "gy")))
    return jax.shard_map(
        per_device, mesh=mesh, in_specs=in_specs, out_specs=out_specs, check_vma=False
    )
```

```python
import functools

import jax
import jax.numpy as jnp
import ml_dtypes
import numpy as np
from jax import lax
from jax.experimental import pallas as pl
from jax.experimental.pallas import tpu as pltpu
from jax.sharding import PartitionSpec as P

UL = 10
NWL = 10
NCLS = 10
WIDTH = 3
GROUP = 8
CHUNKS = 2
PIECE = 512
UNROLL = 2
DIVISORS = (3.0, 2.0, 1.0)
HIGH = (1, -8, 37, 37, -8, 1)
DAMP = (-1, 5, -10, 10, -5, 1)

heat_coef = 0.5
wall_coef = 0.05
conduct = 0.3
inner_coef = 0.2
room_coef = 0.1
flux_coef = 0.5
face_scale = 0.5 / 60.0


def lane_index(shape):
    return lax.broadcasted_iota(jnp.int32, shape, 1)


def rolled(array, shift):
    return pltpu.roll(array, shift % array.shape[1], 1)


def pack_edges(packed, row, x):
    moved = rolled(row, GROUP * x + WIDTH)
    lane = lane_index(row.shape)
    here = (lane >= GROUP * x) & (lane < GROUP * x + 2 * WIDTH)
    return moved if packed is None else jnp.where(here, moved, packed)


def ahead(row, halo, lane, k):
    if k > 0:
        return rolled(jnp.where(lane < k, halo, row), -k)
    return rolled(jnp.where(lane >= row.shape[1] + k, halo, row), -k)


def even_index(axis):
    return lax.rem(lax.axis_index(axis), 2) == 0


def first_rows_kernel(x_size, rows, levels, pieces, field, wind, to_a, to_b, field_here, wind_here, sems):
    size = rows * x_size // pieces
    copies = [
        pltpu.make_async_copy(field.at[pl.ds(p * size, size), :], field_here.at[pl.ds(p * size, size), :], sems.at[p])
        for p in range(pieces)
    ]
    copies.append(pltpu.make_async_copy(wind.at[pl.ds(0, levels * x_size), :], wind_here, sems.at[pieces]))
    for copy in copies:
        copy.start()
    even = even_index("gx")
    for p in range(pieces):
        copies[p].wait()
        for t in range(p * rows // pieces // 8, (p + 1) * rows // pieces // 8):
            for j in range(WIDTH):
                low = field_here[pl.ds(t * 8 * x_size + j, 8, stride=x_size), :]
                high = field_here[pl.ds(t * 8 * x_size + x_size - WIDTH + j, 8, stride=x_size), :]
                to_a[j * rows + t * 8 : j * rows + t * 8 + 8, :] = jnp.where(even, high, low)
                to_b[j * rows + t * 8 : j * rows + t * 8 + 8, :] = jnp.where(even, low, high)
    copies[pieces].wait()
    for t in range(levels // 8):
        low = wind_here[pl.ds(t * 8 * x_size, 8, stride=x_size), :]
        high = wind_here[pl.ds(t * 8 * x_size + x_size - 1, 8, stride=x_size), :]
        at = WIDTH * rows + t * 8
        to_a[at : at + 8, :] = jnp.where(even, high, low)
        to_b[at : at + 8, :] = jnp.where(even, low, high)


def extract_kernel(x_size, chunk, with_wind, field, *refs):
    if with_wind:
        wind, packed = refs
    else:
        to_a, to_b, packed = refs
    rows = packed.shape[0]
    if with_wind:
        levels = wind.shape[0] // (2 * x_size)
        rows = rows - levels
    even = even_index("gx")

    def one(t, carry):
        base = pl.multiple_of((chunk * rows + t * 8) * x_size, 8 * x_size)
        edges = None
        for x in range(x_size):
            edges = pack_edges(edges, field[pl.ds(base + x, 8, stride=x_size), :], x)
        packed[pl.ds(pl.multiple_of(t * 8, 8), 8), :] = edges
        if not with_wind:
            for j in range(WIDTH):
                low = field[pl.ds(base + j, 8, stride=x_size), :]
                high = field[pl.ds(base + x_size - WIDTH + j, 8, stride=x_size), :]
                at = pl.ds(pl.multiple_of(j * rows + t * 8, 8), 8)
                to_a[at, :] = jnp.where(even, high, low)
                to_b[at, :] = jnp.where(even, low, high)
        return carry

    lax.fori_loop(0, rows // 8, one, 0, unroll=4)
    if with_wind:

        def one_wind(t, carry):
            base = pl.multiple_of((levels + t * 8) * x_size, 8 * x_size)
            edges = None
            for x in range(x_size):
                edges = pack_edges(edges, wind[pl.ds(base + x, 8, stride=x_size), :], x)
            packed[pl.ds(pl.multiple_of(rows + t * 8, 8), 8), :] = edges
            return carry

        lax.fori_loop(0, levels // 8, one_wind, 0, unroll=4)


def join_packs(even, from_a, from_b):
    south = jnp.where(even, from_b, from_a)
    north = jnp.where(even, from_a, from_b)
    return jnp.where((lane_index(south.shape) & (GROUP - 1)) < WIDTH, south, north)


def wind_kernel(x_size, rows, wind, factor, pack_a, pack_b, *outs):
    speed_x, ahead_y, behind_y, edge_ahead, edge_behind, scales = outs
    levels = speed_x.shape[1]
    even_y = even_index("gy")
    for x in range(x_size):
        mapped = factor[pl.ds(x, 1), :]
        for k, divisor in enumerate(DIVISORS):
            scales[k, x] = jnp.broadcast_to(mapped * mapped * (-1.0 / divisor), scales.shape[2:])

    def one(t, carry):
        base = pl.multiple_of(t * 8 * x_size, 8 * x_size)
        at = pl.ds(pl.multiple_of(t * 8, 8), 8)
        before = jnp.zeros((8, wind.shape[1]), jnp.float32)
        for x in range(x_size + 1):
            now = jnp.zeros_like(before) if x == x_size else wind[pl.ds(base + x, 8, stride=x_size), :]
            speed_x[x, at, :] = face_scale * (before + now)
            before = now
        base = base + levels * x_size
        lane = lane_index(before.shape)
        there = pl.ds(pl.multiple_of(rows + t * 8, 8), 8)
        halo = join_packs(even_y, pack_a[there, :], pack_b[there, :])
        forward, backward = None, None
        for x in range(x_size):
            row = wind[pl.ds(base + x, 8, stride=x_size), :]
            edge = rolled(halo, -(GROUP * x + WIDTH))
            front = face_scale * (row + ahead(row, edge, lane, 1))
            back = face_scale * (row + ahead(row, edge, lane, -1))
            ahead_y[x, at, :] = front
            behind_y[x, at, :] = back
            forward = pack_edges(forward, front, x)
            backward = pack_edges(backward, back, x)
        edge_ahead[at, :] = forward
        edge_behind[at, :] = backward
        return carry

    lax.fori_loop(0, levels // 8, one, 0, unroll=UNROLL)


def stencil_matrices(y_size):
    inner = np.zeros((y_size, 4 * y_size), np.float32)
    edges = np.zeros((y_size, 4 * y_size), np.float32)
    for part, (taps, offset) in enumerate(((HIGH, -2), (DAMP, -2), (HIGH, -3), (DAMP, -3))):
        for n, tap in enumerate(taps):
            k = n + offset
            for j in range(y_size):
                if 0 <= j + k < y_size:
                    inner[j + k, part * y_size + j] = tap
            for g in range(0, y_size, GROUP):
                for j in range(WIDTH):
                    if j + k < 0:
                        edges[g + WIDTH + j + k, part * y_size + g + WIDTH + j] = tap
                    if j - WIDTH + k >= 0:
                        edges[g + j + k, part * y_size + g + j] = tap
    return [jnp.asarray(np.concatenate([m, m]).astype(ml_dtypes.bfloat16)) for m in (inner, edges)]


def split_halves(values):
    leading = values.astype(jnp.bfloat16)
    trailing = (values - leading.astype(jnp.float32)).astype(jnp.bfloat16)
    return jnp.concatenate([leading, trailing], axis=1)


def stencil_product(halves, matrix, columns=slice(None)):
    return jnp.dot(halves, matrix[:, columns], preferred_element_type=jnp.float32)


def linear_parts(
    x_size, first, section, corner, here, levels, pack_a, pack_b, after_y, edge_ahead, edge_behind,
    inner_matrix, edge_matrix, share, parts,
):
    y_size = section.shape[-1]
    for p in range(levels * x_size // PIECE):
        n = PIECE // levels
        if first:
            lines = [section[pl.ds(corner + x, levels, stride=x_size), :] for x in range(p * n, (p + 1) * n)]
            values = jnp.concatenate(lines, axis=0)
        else:
            values = section[p * n : (p + 1) * n, pl.ds(here, levels), :].reshape(PIECE, y_size)
        halves = split_halves(values)
        for pair in range(2):
            product = stencil_product(halves, inner_matrix, slice(2 * pair * y_size, 2 * (pair + 1) * y_size))
            for j, part in enumerate(parts[2 * pair : 2 * pair + 2]):
                part[p * PIECE : (p + 1) * PIECE, :] = product[:, j * y_size : (j + 1) * y_size]
    halo = join_packs(after_y, pack_a[pl.ds(here, levels), :], pack_b[pl.ds(here, levels), :])
    product = stencil_product(split_halves(halo), edge_matrix)
    after, before = edge_ahead[...], edge_behind[...]
    share[...] = (
        after * product[:, :y_size]
        - jnp.abs(after) * product[:, y_size : 2 * y_size]
        - before * product[:, 2 * y_size : 3 * y_size]
        + jnp.abs(before) * product[:, 3 * y_size :]
    )


def south_north(x, at, edge_share, edge_lane, levels, ahead_y, behind_y, parts):
    lines = [part[pl.ds(pl.multiple_of(x * levels, levels) + at.start, 8), :] for part in parts]
    after, before = ahead_y[x, at, :], behind_y[x, at, :]
    moved = rolled(edge_share, -(GROUP * x + WIDTH))
    return (
        (after * lines[0] - jnp.abs(after) * lines[1])
        - (before * lines[2] - jnp.abs(before) * lines[3])
        + jnp.where(edge_lane, moved, 0.0)
    )


def south_north_kernel(
    section, pack_a, pack_b, ahead_y, behind_y, edge_ahead, edge_behind, inner_matrix, edge_matrix, out, share, *parts
):
    x_size, chunk_rows, y_size = section.shape
    levels = edge_ahead.shape[0]
    after_y = even_index("gy")

    def block(g, carry):
        here = pl.multiple_of(g * levels, levels)
        linear_parts(
            x_size, False, section, None, here, levels, pack_a, pack_b, after_y, edge_ahead, edge_behind,
            inner_matrix, edge_matrix, share, parts,
        )

        def one(t, carry):
            at = pl.ds(pl.multiple_of(t * 8, 8), 8)
            lane = lane_index((8, y_size))
            edge_lane = (lane < WIDTH) | (lane >= y_size - WIDTH)
            edge_share = share[at, :]
            for x in range(x_size):
                out[x, pl.ds(pl.multiple_of(here + t * 8, 8), 8), :] = south_north(
                    x, at, edge_share, edge_lane, levels, ahead_y, behind_y, parts
                )
            return carry

        lax.fori_loop(0, levels // 8, one, 0, unroll=UNROLL)
        return carry

    lax.fori_loop(0, chunk_rows // levels, block, 0)


def section_kernel(x_size, k, chunk, last, with_city, split, *refs):
    refs = list(refs)
    first = k == 0
    section = refs.pop(0)
    base_ref = section if first else refs.pop(0)
    from_a, from_b, pack_a, pack_b = [refs.pop(0) for _ in range(4)]
    wind_a, wind_b = [refs.pop(0) for _ in range(2)]
    speed_x, ahead_y, behind_y, edge_ahead, edge_behind, scales = [refs.pop(0) for _ in range(6)]
    inner_matrix, edge_matrix = [refs.pop(0) for _ in range(2)]
    if split:
        turned = refs.pop(0)
    else:
        parts = refs[-4:]
        share = refs[-5]
        refs = refs[:-5]
    if last:
        if with_city:
            city = [refs.pop(0) for _ in range(6)]
            out, wall_out, indoor_out = refs
        else:
            refs.pop(0)
            (out,) = refs
    else:
        out, to_a, to_b, packed = refs
    levels, y_size = edge_ahead.shape
    chunk_rows = base_ref.shape[0] // (CHUNKS * x_size)
    even_x, after_y = even_index("gx"), even_index("gy")

    def block(g, carry):
        corner = pl.multiple_of((chunk * chunk_rows + g * levels) * x_size, levels * x_size)
        here = pl.multiple_of(g * levels, levels)
        if not split:
            linear_parts(
                x_size, first, section, corner, here, levels, pack_a, pack_b, after_y, edge_ahead, edge_behind,
                inner_matrix, edge_matrix, share, parts,
            )

        def one(t, carry):
            at = pl.ds(pl.multiple_of(t * 8, 8), 8)
            rows_at = pl.ds(pl.multiple_of(here + t * 8, 8), 8)
            start = pl.multiple_of(corner + t * 8 * x_size, 8 * x_size)

            def halo_rows(mine, other, j):
                edge_at = pl.ds(pl.multiple_of(j * chunk_rows + here + t * 8, 8), 8)
                return jnp.where(even_x, mine[edge_at, :], other[edge_at, :])

            def outer_wind(mine, other):
                wind_at = pl.ds(pl.multiple_of(WIDTH * chunk_rows + t * 8, 8), 8)
                return jnp.where(even_x, mine[wind_at, :], other[wind_at, :])

            def cell(x):
                if x < 0:
                    return halo_rows(from_b, from_a, x + WIDTH)
                if x >= x_size:
                    return halo_rows(from_a, from_b, x - x_size)
                return section[pl.ds(start + x, 8, stride=x_size), :] if first else section[x, rows_at, :]

            lane = lane_index((8, y_size))
            edge_lane = (lane < WIDTH) | (lane >= y_size - WIDTH)
            edge_share = None if split else share[at, :]
            q = [cell(x) for x in range(-3, 2)]
            d1 = [q[i + 1] - q[i] for i in range(4)]
            d2 = [d1[i + 1] - d1[i] for i in range(3)]
            d3 = [d2[i + 1] - d2[i] for i in range(2)]
            d4 = d3[1] - d3[0]
            smooth = d4 - 5.0 * d2[1] + 30.0 * q[2]
            q, d1, d2, d3 = q[3:], d1[-1], d2[-1], d3[-1]
            flux_before = None
            edges, lows = None, []
            for x in range(-1, x_size):
                q.append(cell(x + WIDTH))
                new1 = q[-1] - q[-2]
                new2 = new1 - d1
                new3 = new2 - d2
                new4 = new3 - d3
                new_smooth = new4 - 5.0 * d2 + 30.0 * q[0]
                speed = speed_x[x + 1, at, :]
                if x == -1:
                    speed = speed + face_scale * outer_wind(wind_b, wind_a)
                if x == x_size - 1:
                    speed = speed + face_scale * outer_wind(wind_a, wind_b)
                flux = speed * (smooth + new_smooth) - jnp.abs(speed) * (new4 - d4)
                d1, d2, d3, d4, smooth = new1, new2, new3, new4, new_smooth
                if x >= 0:
                    if split:
                        turn = turned[x, rows_at, :]
                    else:
                        turn = south_north(x, at, edge_share, edge_lane, levels, ahead_y, behind_y, parts)
                    divergence = (flux - flux_before) + turn
                    base = base_ref[pl.ds(start + x, 8, stride=x_size), :]
                    new = base + scales[k, x] * divergence
                    if last:
                        out[pl.ds(pl.multiple_of(t * 8 * x_size, 8 * x_size) + x, 8, stride=x_size), :] = new
                    else:
                        out[x, rows_at, :] = new
                        edges = pack_edges(edges, new, x)
                        if x < WIDTH:
                            lows.append(new)
                        if x >= x_size - WIDTH:
                            j = x - x_size + WIDTH
                            edge_at = pl.ds(pl.multiple_of(j * chunk_rows + here + t * 8, 8), 8)
                            to_a[edge_at, :] = jnp.where(even_x, new, lows[j])
                            to_b[edge_at, :] = jnp.where(even_x, lows[j], new)
                flux_before = flux
                q = q[1:]
            if not last:
                packed[rows_at, :] = edges
            return carry

        lax.fori_loop(0, levels // 8, one, 0, unroll=UNROLL)
        return carry

    if last:
        block(pl.program_id(0), 0)
    else:
        lax.fori_loop(0, chunk_rows // levels, block, 0)
    if last and with_city:

        @pl.when(pl.program_id(0) == 0)
        def _():
            city_step(x_size, out, *city, wall_out, indoor_out)


def dot(a, b, dims):
    return lax.dot_general(
        a, b, (dims, ((), ())), precision=lax.Precision.HIGHEST, preferred_element_type=jnp.float32
    )


def city_step(x_size, out, counts, cols_ref, class_ref, table, wall_ref, indoor_ref, wall_out, indoor_out):
    deep = 16
    cols = cols_ref[...]
    slots = cols.shape[1]
    y_size = out.shape[1]
    cell_x = lax.div(cols, y_size)
    cell_y = lax.rem(cols, y_size)
    lower = [
        jnp.concatenate([out[pl.ds(8 * x_size * t + x, 8, stride=x_size), :] for t in range(deep // 8)], axis=0)
        for x in range(x_size)
    ]
    at_y = (lax.broadcasted_iota(jnp.int32, (y_size, slots), 0) == cell_y).astype(jnp.float32)
    gathered = dot(jnp.concatenate(lower, axis=0), at_y, ((1,), (0,)))
    air = jnp.zeros((deep, slots), jnp.float32)
    for x in range(x_size):
        air = jnp.where(cell_x == x, gathered[deep * x : deep * (x + 1)], air)
    air = air[:UL]
    onehot = (lax.broadcasted_iota(jnp.int32, (NCLS, slots), 0) == class_ref[...]).astype(jnp.float32)
    areas = dot(table[...], onehot, ((0,), (0,)))
    walls = wall_ref[...]
    indoor = indoor_ref[...]
    heat = heat_coef * areas * (walls[0:1] - air)
    wall_first = walls[0:1] - wall_coef * jnp.sum(heat, axis=0, keepdims=True) + conduct * (walls[1:2] - walls[0:1])
    middle = walls[1:-1] + conduct * (walls[:-2] - 2.0 * walls[1:-1] + walls[2:])
    last = walls[-1:] + conduct * (walls[-2:-1] - walls[-1:]) + inner_coef * (indoor - walls[-1:])
    indoor_new = indoor + room_coef * (walls[-1:] - indoor)
    live = lax.broadcasted_iota(jnp.int32, (1, slots), 1) < counts[0]
    wall_out[...] = jnp.where(live, jnp.concatenate([wall_first, middle, last], axis=0), walls)
    indoor_out[...] = jnp.where(live, indoor_new, indoor)
    heating = jnp.where(live, flux_coef * heat, 0.0)
    heating = jnp.concatenate([heating, jnp.zeros((deep - UL, slots), jnp.float32)], axis=0)
    spread = jnp.concatenate([jnp.where(cell_x == x, heating, 0.0) for x in range(x_size)], axis=0)
    added = dot(spread, at_y, ((1,), (1,)))
    for x in range(x_size):
        for t in range(deep // 8):
            out[pl.ds(8 * x_size * t + x, 8, stride=x_size), :] = (
                lower[x][8 * t : 8 * t + 8] + added[deep * x + 8 * t : deep * x + 8 * t + 8]
            )


def exchange(axis, to_a, to_b):
    size = lax.axis_size(axis)
    pairs_a = [(i, i + 1) for i in range(0, size, 2)]
    pairs_b = [(i, (i + 1) % size) for i in range(1, size, 2)]
    both = [pairs + [(j, i) for i, j in pairs] for pairs in (pairs_a, pairs_b)]
    return lax.ppermute(to_a, axis, both[0]), lax.ppermute(to_b, axis, both[1])


def per_device(
    scalars,
    winds,
    map_factor,
    urban_counts,
    urban_cols,
    street_class,
    area_table,
    wall_temp,
    indoor_temp,
):
    n_scalars, levels, x_size, y_size = scalars.shape
    slots = urban_cols.shape[0]
    rows = n_scalars * levels // CHUNKS
    f32 = functools.partial(jax.ShapeDtypeStruct, dtype=jnp.float32)
    field = scalars.reshape(n_scalars * levels * x_size, y_size)
    wind = winds.reshape(2 * levels * x_size, y_size)
    params = pltpu.CompilerParams(vmem_limit_bytes=40 * 2**20)
    whole = pl.BlockSpec(memory_space=pltpu.VMEM)

    smem = pl.BlockSpec(memory_space=pltpu.SMEM)
    hbm = pl.BlockSpec(memory_space=pltpu.HBM)
    cheap = pl.CostEstimate(flops=1000, bytes_accessed=1000, transcendentals=0)

    pieces = 4
    first_rows = pl.pallas_call(
        functools.partial(first_rows_kernel, x_size, rows, levels, pieces),
        in_specs=[hbm, hbm],
        out_specs=[whole] * 2,
        out_shape=[f32((WIDTH * rows + levels, y_size))] * 2,
        scratch_shapes=[
            pltpu.VMEM((rows * x_size, y_size), jnp.float32),
            pltpu.VMEM((levels * x_size, y_size), jnp.float32),
            pltpu.SemaphoreType.DMA((pieces + 1,)),
        ],
        compiler_params=pltpu.CompilerParams(vmem_limit_bytes=62 * 2**20),
        cost_estimate=cheap,
        name="first_rows",
    )(field, wind)
    received = [None] * CHUNKS
    received[0] = exchange("gx", *first_rows)
    for c in range(CHUNKS):
        extra = levels if c == 0 else 0
        outs = pl.pallas_call(
            functools.partial(extract_kernel, x_size, c, c == 0),
            in_specs=[whole] + [whole] * (c == 0),
            out_specs=[whole] * (1 if c == 0 else 3),
            out_shape=[f32((WIDTH * rows, y_size))] * (0 if c == 0 else 2) + [f32((rows + extra, y_size))],
            compiler_params=params,
            cost_estimate=cheap,
            name=f"extract_{c}",
        )(field, *([wind] if c == 0 else []))
        if c > 0:
            received[c] = exchange("gx", *outs[:2])
        received[c] = (*received[c], *exchange("gy", outs[-1], outs[-1]))

    speeds = pl.pallas_call(
        functools.partial(wind_kernel, x_size, rows),
        in_specs=[whole] * 4,
        out_specs=[whole] * 6,
        out_shape=[
            f32((x_size + 1, levels, y_size)),
            f32((x_size, levels, y_size)),
            f32((x_size, levels, y_size)),
            f32((levels, y_size)),
            f32((levels, y_size)),
            f32((len(DIVISORS), x_size, 8, y_size)),
        ],
        compiler_params=params,
        cost_estimate=cheap,
        name="speeds",
    )(wind, map_factor, *received[0][2:])
    winds_beyond = received[0][:2]
    matrices = stencil_matrices(y_size)

    steps = rows // levels
    sections = [None] * CHUNKS
    result = None
    for k in range(len(DIVISORS)):
        last = k == len(DIVISORS) - 1
        for c in range(CHUNKS):
            operands = [field] if k == 0 else [sections[c], field]
            operands += [*received[c], *winds_beyond, *speeds, *matrices]
            specs = [whole] * len(operands)
            city = last and c == 0
            split = last and c == CHUNKS - 1
            scratch = [pltpu.VMEM((levels, y_size), jnp.float32)]
            scratch += [pltpu.VMEM((levels * x_size, y_size), jnp.float32)] * 4
            if split:
                tied, indoor_out = lax.optimization_barrier((sections[c], indoor_out))
                turned = pl.pallas_call(
                    south_north_kernel,
                    in_specs=[whole] * 9,
                    out_specs=whole,
                    out_shape=f32((x_size, rows, y_size)),
                    scratch_shapes=scratch,
                    compiler_params=params,
                    cost_estimate=cheap,
                    name="south_north",
                )(tied, *received[c][2:], *speeds[1:5], *matrices)
                operands += [turned]
                specs += [whole]
                scratch = []
            aliases = {}
            flat_c = pl.BlockSpec((levels * x_size, y_size), lambda g, c=c: (c * steps + g, 0))
            if city:
                operands += [
                    urban_counts,
                    urban_cols[None],
                    street_class[None],
                    area_table,
                    wall_temp,
                    indoor_temp[None],
                ]
                specs += [smem] + [whole] * 5
                out_specs = [flat_c, whole, whole]
                out_shape = [f32(field.shape), f32(wall_temp.shape), f32((1, slots))]
            elif last:
                aliases = {len(operands): 0}
                operands += [result]
                specs += [pl.BlockSpec(memory_space=pl.ANY)]
                out_specs = [flat_c]
                out_shape = [f32(field.shape)]
            else:
                out_specs = [whole] * 4
                out_shape = [
                    f32((x_size, rows, y_size)),
                    f32((WIDTH * rows, y_size)),
                    f32((WIDTH * rows, y_size)),
                    f32((rows, y_size)),
                ]
            outs = pl.pallas_call(
                functools.partial(section_kernel, x_size, k, c, last, city, split),
                grid=(steps,) if last else (),
                in_specs=specs,
                out_specs=out_specs,
                out_shape=out_shape,
                scratch_shapes=scratch,
                input_output_aliases=aliases,
                compiler_params=params,
                cost_estimate=cheap,
                name=f"section_{k}_{c}",
            )(*operands)
            if city:
                result, wall_out, indoor_out = outs
            elif last:
                (result,) = outs
            else:
                sections[c], *outgoing, packed = outs
                received[c] = (*exchange("gx", *outgoing), *exchange("gy", packed, packed))
    return (result.reshape(scalars.shape), wall_out, indoor_out[0])


def solution(mesh):
    in_specs = (
        P(None, None, "gx", "gy"),
        P(None, None, "gx", "gy"),
        P("gx", "gy"),
        P(("gx", "gy")),
        P(("gx", "gy")),
        P(("gx", "gy")),
        P(),
        P(None, ("gx", "gy")),
        P(("gx", "gy")),
    )
    out_specs = (P(None, None, "gx", "gy"), P(None, ("gx", "gy")), P(("gx", "gy")))
    return jax.shard_map(
        per_device, mesh=mesh, in_specs=in_specs, out_specs=out_specs, check_vma=False
    )
```
